32 devices in a mesh: slab: 8 (over y, x, core), shots: 4 (over z).
Axes of the slice: x: 2, y: 2, z: 4, core: 2. Of those that a mesh axis runs over, the one named last changes fastest.
Arguments:
- src_prev: float32 [8, 64, 64, 128], P('shots', 'slab'), may hold values from -6 to 6
- src_cur: float32 [8, 64, 64, 128], P('shots', 'slab'), may hold values from -6 to 6
- rcv_prev: float32 [8, 64, 64, 128], P('shots', 'slab'), may hold values from -6 to 6
- rcv_cur: float32 [8, 64, 64, 128], P('shots', 'slab'), may hold values from -6 to 6
- velocity: float32 [64, 64, 128], P('slab'), may hold values from 0.05 to 0.18
- wavelet: float32 [2, 8], P(None, 'shots'), may hold values from -6 to 6
- residual_traces: float32 [2, 8, 256], P(None, 'shots'), may hold values from -6 to 6
- source_depth: int32 [8], P('shots'), may hold values from 0 to 63
- source_y: int32 [8], P('shots'), may hold values from 21 to 42
- source_x: int32 [8], P('shots'), may hold values from 42 to 85
- half_y: int32 [8], P('shots'), may hold values from 10 to 21
- half_x: int32 [8], P('shots'), may hold values from 21 to 42
- receiver_cell: int32 [8, 256], P('shots'), may hold values from 0 to 524287
Outputs:
- src_last: float32 [8, 64, 64, 128], P('shots', 'slab')
- rcv_last: float32 [8, 64, 64, 128], P('shots', 'slab')
- image: float32 [64, 64, 128], P('slab')
The draws below stay inside these ranges and needn't reach their ends.
All inputs are finite; a program needn't handle non-finite values.
Results may differ from the reference program's by a relative error of at most 0.0003.
Values sent between devices are 32-bit elements; how exact they have to be, the bound alone decides.
No kernel may reach another device: no remote copies, remote signals or barrier semaphores. Data moves between devices by JAX's collectives and lax.ppermute only.
A program may use at most 64 MiB of HBM per device.

```python
import jax
import jax.numpy as jnp
from jax import lax

NY = 64
NX = 128
RCV = 256
STEPS = 2
NZ = 64
SHOTS = 8


def with_ends(entries, rng, low, high):
    longest = entries.shape.index(max(entries.shape))
    spots = []
    for shift in (0, 1):
        where = [jax.random.randint(jax.random.fold_in(rng, axis), (), 0, length) for axis, length in enumerate(entries.shape)]
        where[longest] = (where[longest] + shift) % entries.shape[longest]
        spots.append(tuple(where))
    return entries.at[spots[0]].set(low).at[spots[1]].set(high)


def block_scale(own_key, extent, shards, low, top_value):
    def one(dim, parts):
        heights = jax.random.uniform(jax.random.fold_in(jax.random.fold_in(own_key, 6), dim), (parts,), jnp.float32, low / len(shards), top_value / len(shards))
        return jnp.repeat(jnp.exp(heights), extent[dim] // parts).reshape((-1,) + (1,) * (len(extent) - dim - 1))

    level = one(*shards[0])
    for cut in shards[1:]:
        level = level * one(*cut)
    return level


def normal_values(stream_key, shape, spread, reach, pieces=(), kind=jnp.bfloat16):
    result = jax.random.normal(stream_key, shape, jnp.float32) * spread
    if len(pieces) > 0:
        result = block_scale(stream_key, shape, pieces, -0.22, 0.18) * result
    return jnp.clip(result, min=-reach, max=reach).astype(kind)


def setup_inputs(seed: int = 0) -> dict:
    streams_of = jax.random.split(jax.random.key(seed), 14)
    src_prev = normal_values(streams_of[0], (SHOTS, NZ, NY, NX), 1.0, 6.0, ((0, 4), (1, 8)), jnp.float32)
    src_cur = normal_values(streams_of[1], (SHOTS, NZ, NY, NX), 1.0, 6.0, ((0, 4), (1, 8)), jnp.float32)
    rcv_prev = normal_values(streams_of[2], (SHOTS, NZ, NY, NX), 1.0, 6.0, ((0, 4), (1, 8)), jnp.float32)
    rcv_cur = normal_values(streams_of[3], (SHOTS, NZ, NY, NX), 1.0, 6.0, ((0, 4), (1, 8)), jnp.float32)
    velocity = jnp.clip(0.05 + 0.13000001 * jax.random.uniform(streams_of[4], (NZ, NY, NX), jnp.float32) ** block_scale(streams_of[4], (NZ, NY, NX), ((0, 8),), -0.2, 0.2), 0.05, 0.18)
    wavelet = normal_values(streams_of[5], (STEPS, SHOTS), 1.0, 6.0, ((1, 4),), jnp.float32)
    residual_traces = normal_values(streams_of[6], (STEPS, SHOTS, RCV), 1.0, 6.0, ((1, 4),), jnp.float32)
    source_depth = with_ends(jax.random.randint(streams_of[7], (SHOTS,), 0, NZ), jax.random.fold_in(streams_of[7], 1), 0, NZ - 1).astype(jnp.int32)
    source_y = with_ends(jax.random.randint(streams_of[8], (SHOTS,), NY // 3, NY - NY // 3), jax.random.fold_in(streams_of[8], 1), NY // 3, (NY - NY // 3) - 1).astype(jnp.int32)
    source_x = with_ends(jax.random.randint(streams_of[9], (SHOTS,), NX // 3, NX - NX // 3), jax.random.fold_in(streams_of[9], 1), NX // 3, (NX - NX // 3) - 1).astype(jnp.int32)
    half_y = with_ends(jax.random.randint(streams_of[10], (SHOTS,), NY // 6, NY // 3 + 1), jax.random.fold_in(streams_of[10], 1), NY // 6, (NY // 3 + 1) - 1).astype(jnp.int32)
    half_x = with_ends(jax.random.randint(streams_of[11], (SHOTS,), NX // 6, NX // 3 + 1), jax.random.fold_in(streams_of[11], 1), NX // 6, (NX // 3 + 1) - 1).astype(jnp.int32)
    receiver_cell = with_ends(jax.random.randint(streams_of[12], (SHOTS, RCV), 0, NZ * NY * NX), jax.random.fold_in(streams_of[12], 1), 0, (NZ * NY * NX) - 1).astype(jnp.int32)
    return dict(src_prev=src_prev, src_cur=src_cur, rcv_prev=rcv_prev, rcv_cur=rcv_cur, velocity=velocity, wavelet=wavelet, residual_traces=residual_traces, source_depth=source_depth, source_y=source_y, source_x=source_x, half_y=half_y, half_x=half_x, receiver_cell=receiver_cell)


COEF = (-205.0 / 72.0, 8.0 / 5.0, -1.0 / 5.0, 8.0 / 315.0, -1.0 / 560.0)


def laplace(padded):
    axis_z = padded.ndim - 3
    length = padded.shape[axis_z] - 8
    center = lax.slice_in_dim(padded, 4, 4 + length, axis=axis_z)
    total = 3.0 * COEF[0] * center
    for shift_k in range(1, 5):
        upper = lax.slice_in_dim(padded, 4 + shift_k, 4 + shift_k + length, axis=axis_z)
        lower = lax.slice_in_dim(padded, 4 - shift_k, 4 - shift_k + length, axis=axis_z)
        total = total + COEF[shift_k] * (upper + lower)
    widths = [(0, 0)] * (center.ndim - 2) + [(4, 4), (4, 4)]
    plane = jnp.pad(center, widths)
    rows_y = center.shape[-2]
    cols_x = center.shape[-1]
    for shift_k in range(1, 5):
        side_y = plane[..., 4 + shift_k:4 + shift_k + rows_y, 4:4 + cols_x] + plane[..., 4 - shift_k:4 - shift_k + rows_y, 4:4 + cols_x]
        side_x = plane[..., 4:4 + rows_y, 4 + shift_k:4 + shift_k + cols_x] + plane[..., 4:4 + rows_y, 4 - shift_k:4 - shift_k + cols_x]
        total = total + COEF[shift_k] * (side_y + side_x)
    return total


def band_mask(source_y, source_x, half_y, half_x, rows_y, cols_x):
    grid_y = jnp.arange(rows_y, dtype=jnp.int32)
    grid_x = jnp.arange(cols_x, dtype=jnp.int32)
    inside_y = jnp.abs(grid_y[None, :, None] - source_y[:, None, None]) <= half_y[:, None, None]
    inside_x = jnp.abs(grid_x[None, None, :] - source_x[:, None, None]) <= half_x[:, None, None]
    return (inside_y & inside_x).astype(jnp.float32)


def inject(cells, values, begin, length, rows_y, cols_x):
    plane = rows_y * cols_x
    depth = cells // plane
    rest = cells - depth * plane
    local = depth - begin
    valid = (local >= 0) & (local < length)
    flat = jnp.where(valid, local * plane + rest, 0).astype(jnp.int32)
    amounts = jnp.where(valid, values, jnp.zeros_like(values))
    count = cells.shape[0]
    rows = jnp.broadcast_to(jnp.arange(count, dtype=jnp.int32)[:, None], flat.shape)
    field = jnp.zeros((count, length * plane), jnp.float32).at[rows, flat].add(amounts)
    return field.reshape(count, length, rows_y, cols_x)


def one_shot(items, velocity):
    up, u, vp, v, wave, traces, sdepth, sy, sx, hy, hx, rcells = items
    up, u, vp, v = up[None], u[None], vp[None], v[None]
    depth_all, rows_y, cols_x = velocity.shape
    mask = band_mask(sy[None], sx[None], hy[None], hx[None], rows_y, cols_x)[:, None]
    scell = (sdepth * rows_y * cols_x + sy * cols_x + sx)[None, None]
    image = jnp.zeros(velocity.shape, jnp.float32)
    for step in range(STEPS):
        both = jnp.pad(jnp.stack([u, v]), [(0, 0), (0, 0), (4, 4), (0, 0), (0, 0)])
        lap = laplace(both)
        sdelta = inject(scell, wave[step][None, None], 0, depth_all, rows_y, cols_x)
        rdelta = inject(rcells[None], traces[step][None], 0, depth_all, rows_y, cols_x)
        unew = mask * (2.0 * u - up + velocity * lap[0] + sdelta)
        vnew = mask * (2.0 * v - vp + velocity * lap[1] + rdelta)
        image = image + jnp.sum((unew - 2.0 * u + up) * vnew, axis=0)
        up, u, vp, v = u, unew, v, vnew
    return u[0], v[0], image


def reference(src_prev, src_cur, rcv_prev, rcv_cur, velocity, wavelet, residual_traces, source_depth, source_y, source_x, half_y, half_x, receiver_cell):
    items = (src_prev, src_cur, rcv_prev, rcv_cur, jnp.swapaxes(wavelet, 0, 1), jnp.swapaxes(residual_traces, 0, 1), source_depth, source_y, source_x, half_y, half_x, receiver_cell)
    src_last, rcv_last, images = lax.map(lambda item: one_shot(item, velocity), items)
    return src_last, rcv_last, jnp.sum(images, axis=0)
```

```python
import functools

import jax
import jax.numpy as jnp
from jax import lax
from jax.experimental import pallas as pl
from jax.experimental.pallas import tpu as pltpu
from jax.sharding import PartitionSpec as P

STEPS = 2
COEF = (-205.0 / 72.0, 8.0 / 5.0, -1.0 / 5.0, 8.0 / 315.0, -1.0 / 560.0)
R = 4
HALF_Y, HALF_X = 21, 42
WIN_Y, WIN_X = 2 * HALF_Y + 1, 2 * HALF_X + 1
PACK = 32
UNPACK = 48
SCALE = 5040.0
MARGIN = 8

VMEM = pl.BlockSpec(memory_space=pltpu.VMEM)
ANY = pl.BlockSpec(memory_space=pl.ANY)
HBM = pl.BlockSpec(memory_space=pltpu.HBM)


def params(**more):
    return pltpu.CompilerParams(vmem_limit_bytes=24 * 1024 * 1024, **more)


def cost(flops, nbytes):
    return pl.CostEstimate(flops=flops, bytes_accessed=nbytes, transcendentals=0)


def parity():
    return lax.rem(lax.axis_index("slab"), 2)


def halves():
    par = parity()
    return par * R, R - par * R


def lanes(shape):
    return lax.broadcasted_iota(jnp.int32, shape, 1)


def sublanes(shape):
    return lax.broadcasted_iota(jnp.int32, shape, 0)


def band(scal, s, shape):
    sy, sx, hy, hx = (ref[s] for ref in scal)
    return (jnp.abs(sublanes(shape) - sy) <= hy) & (jnp.abs(lanes(shape) - sx) <= hx)


def pack(rows, col0):
    cols = rows.shape[1]
    main = pltpu.roll(rows[:PACK], cols - col0, 1)
    left = pltpu.roll(rows[PACK:], lax.rem(WIN_X - col0 + cols, cols), 1)
    right = pltpu.roll(rows[PACK:], lax.rem(HALF_X - col0 + cols, cols), 1)
    return jnp.where(lanes(main.shape) < WIN_X, main, jnp.concatenate([left, right], 0))


def unpack(packed, col0):
    cols = packed.shape[1]
    main = pltpu.roll(packed, col0, 1)
    left = pltpu.roll(packed[: PACK // 2], lax.rem(col0 + cols - WIN_X, cols), 1)
    right = pltpu.roll(packed[PACK // 2 :], lax.rem(col0 + cols - HALF_X, cols), 1)
    rest = jnp.where(lanes(left.shape) < col0 + (cols - WIN_X), left, right)
    return jnp.concatenate([main, rest], 0)


def pack_planes(planes, out, scal, par):
    for f in range(4):
        row0 = scal[0][f % 2] - HALF_Y
        col0 = scal[1][f % 2] - HALF_X
        for d in range(R):
            i = d + par * (R - 1 - 2 * d)
            out[f * R + d] = pack(planes[f, i, pl.ds(row0, UNPACK), :], col0)


def copies_of(pairs, sems):
    copies = [pltpu.make_async_copy(a, b, sems.at[n]) for n, (a, b) in enumerate(pairs)]
    for copy in copies:
        copy.start()
    return copies


def wait(copies):
    for copy in copies:
        copy.wait()


def pack_kernel(sy_in, sx_in, src, rcv, out, far_out, sy, sx, planes, sems):
    par = parity()
    near, far = halves()
    rows = src.shape[2]
    pairs = [(sy_in, sy), (sx_in, sx)]
    for f in range(4):
        ref = (src, rcv)[f // 2].at[f % 2]
        pairs.append((ref.at[pl.ds(near, R)], planes.at[f, :, pl.ds(0, rows), :]))
    for f in range(4):
        ref = (src, rcv)[f // 2].at[f % 2]
        pairs.append((ref.at[pl.ds(far, R)], far_out.at[f]))
    copies = copies_of(pairs, sems)
    planes[:, :, rows:, :] = jnp.zeros((4, R, MARGIN, planes.shape[3]), jnp.float32)
    wait(copies[:6])
    pack_planes(planes, out, (sy, sx), par)
    wait(copies[6:])


def band_matrix(out):
    cols = out.shape[1]
    apart = jnp.abs(sublanes((cols, cols)) - lanes((cols, cols)))
    weights = jnp.zeros((cols, cols), jnp.float32)
    for k in range(1, R + 1):
        weights = jnp.where(apart == k, round(COEF[k] * SCALE) * 1.0, weights)
    for n in range(3):
        out[pl.ds(n * cols, cols)] = weights.astype(jnp.bfloat16)


def x_part(cur, first, matrix, out):
    rows, cols = out.shape[2], out.shape[3]
    for f in range(4):
        rest = cur[f, pl.ds(first + R, R), pl.ds(MARGIN, rows), :].reshape(R * rows, cols)
        parts = []
        for _ in range(3):
            parts.append(rest.astype(jnp.bfloat16))
            rest = rest - parts[-1].astype(jnp.float32)
        total = lax.dot_general(
            jnp.concatenate(parts, 1),
            matrix[...],
            (((1,), (0,)), ((), ())),
            preferred_element_type=jnp.float32,
        )
        out[f] = total.reshape(R, rows, cols)


def laplace(cur, xs, f, i, slot, rows):
    at = lambda layer, row: cur[f, layer, pl.ds(MARGIN + row, rows), :]
    total = 3.0 * COEF[0] * at(slot, 0) + (1.0 / SCALE) * xs[f, i]
    for k in range(1, R + 1):
        side_z = at(slot - k, 0) + at(slot + k, 0)
        side_y = at(slot, -k) + at(slot, k)
        total = total + COEF[k] * (side_z + side_y)
    return total


def inject(cells, traces, step, out, first):
    shots, layers, rows, cols = out.shape
    count = cells.shape[1]
    for s in range(shots):
        flat = cells[pl.ds(s, 1), :]
        line = lax.div(flat, cols)
        col = flat - line * cols
        line = line - first * rows
        spot = sublanes((layers * rows, count)) == line
        spot = jnp.where(spot, 1.0, 0.0).astype(jnp.bfloat16)
        value = jnp.where(sublanes((cols, count)) == col, traces[step, pl.ds(s, 1), :], 0.0)
        total = None
        for _ in range(3):
            part = value.astype(jnp.bfloat16)
            value = value - part.astype(jnp.float32)
            term = lax.dot_general(
                spot, part, (((1,), (1,)), ((), ())), preferred_element_type=jnp.float32
            )
            total = term if total is None else total + term
        out[s] = total.reshape(layers, rows, cols)


def clear(ref, layers):
    fields, slots, tall, cols = ref.shape
    ref[:, :, :MARGIN, :] = jnp.zeros((fields, slots, MARGIN, cols), jnp.float32)
    ref[:, :, tall - MARGIN :, :] = jnp.zeros((fields, slots, MARGIN, cols), jnp.float32)
    if layers is not None:
        ref[:, pl.ds(layers, R), :, :] = jnp.zeros((fields, R, tall, cols), jnp.float32)


def step_half(first, refs, scal, wave, depth, step, base, write):
    cur, prev, vel, delta, matrix, xs = refs
    rows = vel.shape[1]
    x_part(cur, first, matrix, xs)
    for s in range(2):
        spot = (sublanes(vel.shape[1:]) == scal[0][s]) & (lanes(vel.shape[1:]) == scal[1][s])
        here = depth[s] - base

        def layer(i, _):
            p = first + i
            amount = jnp.where(here == p, wave[step, s], 0.0)
            out = []
            for f in (s, 2 + s):
                twice = 2.0 * cur[f, p + R, pl.ds(MARGIN, rows), :] - prev[f, i]
                new = twice + vel[i] * laplace(cur, xs, f, i, p + R, rows)
                if f < 2:
                    new = new + jnp.where(spot, amount, 0.0)
                else:
                    new = new + delta[s, i]
                out.append((twice, new))
            write(s, i, out)
            return 0

        lax.fori_loop(0, R, layer, 0)


def writer_far(scal, new_src, new_rcv, image, before):
    shape = image.shape[1:]

    def write(s, i, out):
        inside = band(scal, s, shape)
        new = [jnp.where(inside, n, 0.0) for _, n in out]
        new_src[s, i] = new[0]
        new_rcv[s, i] = new[1]
        term = (new[0] - out[0][0]) * new[1]
        if s == 0:
            image[i] = term if before is None else term + before[i]
        else:
            image[i] = image[i] + term

    return write


def writer_near(part, twice):
    def write(s, i, out):
        part[s, i] = out[0][1]
        part[2 + s, i] = out[1][1]
        twice[s, i] = out[0][0]

    return write


def first_kernel(
    sy_in, sx_in, hy_in, hx_in, depth_in, wave_in,
    src, rcv, src_prev, rcv_prev, halo, vel_in, cells, traces,
    src_out, rcv_out, far_image, near_part, near_twice, near_vel,
    sy, sx, hy, hx, depth, wave, cur, prev, vel, delta, matrix, xs, sems,
):
    scal = (sy, sx, hy, hx)
    par = parity()
    near, far = halves()
    layers, rows = vel_in.shape[0], vel_in.shape[1]
    base = lax.axis_index("slab") * layers
    pairs = list(zip((sy_in, sx_in, hy_in, hx_in, depth_in, wave_in), (sy, sx, hy, hx, depth, wave)))
    for f in range(4):
        now, before = (src, rcv)[f // 2].at[f % 2], (src_prev, rcv_prev)[f // 2].at[f % 2]
        pairs.append((now, cur.at[f, pl.ds(R, layers), pl.ds(MARGIN, rows), :]))
        pairs.append((before, prev.at[f]))
    pairs.append((halo, cur.at[:, pl.ds((layers + R) * (1 - par), R), pl.ds(MARGIN, rows), :]))
    pairs.append((vel_in, vel))
    copies = copies_of(pairs, sems)
    clear(cur, (layers + R) * par)
    band_matrix(matrix)
    inject(cells, traces, 0, delta, base)
    wait(copies)
    has = jnp.where((base == 0) | (lax.axis_index("slab") == lax.axis_size("slab") - 1), 0.0, 1.0)
    near_vel[...] = vel[pl.ds(near, R)] * has

    for first, write in (
        (far, writer_far(scal, src_out, rcv_out, far_image, None)),
        (near, writer_near(near_part, near_twice)),
    ):
        half = lambda ref: ref.at[:, pl.ds(first, R)]
        refs = (cur, half(prev), vel.at[pl.ds(first, R)], half(delta), matrix, xs)
        step_half(first, refs, scal, wave, depth, 0, base, write)


def finish_near(scal, part, twice, halo, vel, planes, write):
    par = parity()
    rows, cols = vel.shape[1], vel.shape[2]
    for f in range(4):
        row0 = scal[0][f % 2] - HALF_Y
        col0 = scal[1][f % 2] - HALF_X
        for e in range(R):
            planes[f, e, pl.ds(row0, UNPACK), :] = unpack(halo[f * R + e], col0)
    for s in range(2):
        inside = band(scal, s, (rows, cols))
        for d in range(R):
            i = d + par * (R - 1 - 2 * d)
            new = []
            for f in (s, 2 + s):
                side = COEF[d + 1] * planes[f, 0, pl.ds(0, rows), :]
                for k in range(d + 2, R + 1):
                    side = side + COEF[k] * planes[f, k - d - 1, pl.ds(0, rows), :]
                new.append(jnp.where(inside, part[f, i] + vel[i] * side, 0.0))
            write(s, i, new, (new[0] - twice[s, i]) * new[1])


def middle_kernel(
    sy_in, sx_in, hy_in, hx_in, part, twice, halo, vel,
    near_out, near_image, packed,
    sy, sx, hy, hx, planes, sems,
):
    scal = (sy, sx, hy, hx)
    wait(copies_of(zip((sy_in, sx_in, hy_in, hx_in), scal), sems))

    def write(s, i, new, term):
        near_out[s, i] = new[0]
        near_out[2 + s, i] = new[1]
        near_image[i] = term if s == 0 else near_image[i] + term

    finish_near(scal, part, twice, halo, vel, planes, write)
    rows = vel.shape[1]
    planes[:, :, pl.ds(0, rows), :] = near_out[...]
    planes[:, :, rows:, :] = jnp.zeros((4, R, MARGIN, planes.shape[3]), jnp.float32)
    pack_planes(planes, packed, scal, parity())


def second_far_kernel(
    sy_in, sx_in, hy_in, hx_in, depth_in, wave_in,
    src, rcv, near_cur, far_src, far_rcv, halo_src, halo_rcv, vel_in, cells, traces, before,
    src_last, rcv_last, image,
    sy, sx, hy, hx, depth, wave, cur, prev, vel, delta, matrix, xs, new_far, sems,
):
    scal = (sy, sx, hy, hx)
    par = parity()
    near, far = halves()
    layers, rows = vel_in.shape[0], vel_in.shape[1]
    base = lax.axis_index("slab") * layers
    pairs = list(zip((sy_in, sx_in, hy_in, hx_in, depth_in, wave_in), (sy, sx, hy, hx, depth, wave)))
    pairs += [
        (near_cur, cur.at[:, pl.ds(R + near, R), pl.ds(MARGIN, rows), :]),
        (far_src, cur.at[pl.ds(0, 2), pl.ds(R + far, R), pl.ds(MARGIN, rows), :]),
        (far_rcv, cur.at[pl.ds(2, 2), pl.ds(R + far, R), pl.ds(MARGIN, rows), :]),
        (halo_src, cur.at[pl.ds(0, 2), pl.ds((layers + R) * (1 - par), R), pl.ds(MARGIN, rows), :]),
        (halo_rcv, cur.at[pl.ds(2, 2), pl.ds((layers + R) * (1 - par), R), pl.ds(MARGIN, rows), :]),
        (src.at[:, pl.ds(far, R)], prev.at[pl.ds(0, 2)]),
        (rcv.at[:, pl.ds(far, R)], prev.at[pl.ds(2, 2)]),
        (vel_in.at[pl.ds(far, R)], vel),
    ]
    copies = copies_of(pairs, sems)
    clear(cur, None)
    band_matrix(matrix)
    inject(cells, traces, 1, delta, base + far)
    wait(copies)
    refs = (cur, prev, vel, delta, matrix, xs)
    step_half(far, refs, scal, wave, depth, 1, base, writer_far(scal, new_far.at[pl.ds(0, 2)], new_far.at[pl.ds(2, 2)], image, before))
    wait(copies_of([
        (new_far.at[pl.ds(2 * n, 2)], (src_last, rcv_last)[n].at[:, pl.ds(far, R)]) for n in range(2)
    ], sems))


def second_near_kernel(
    sy_in, sx_in, depth_in, wave_in,
    src, rcv, near_cur, far_src, far_rcv, vel_in, cells, traces,
    near_part, near_twice,
    sy, sx, depth, wave, cur, prev, vel, delta, matrix, xs, sems,
):
    scal = (sy, sx)
    par = parity()
    near, far = halves()
    layers, rows = vel_in.shape[0], vel_in.shape[1]
    base = lax.axis_index("slab") * layers
    pairs = list(zip((sy_in, sx_in, depth_in, wave_in), (sy, sx, depth, wave)))
    pairs += [
        (near_cur, cur.at[:, pl.ds(R + near, R), pl.ds(MARGIN, rows), :]),
        (far_src, cur.at[pl.ds(0, 2), pl.ds(R + far, R), pl.ds(MARGIN, rows), :]),
        (far_rcv, cur.at[pl.ds(2, 2), pl.ds(R + far, R), pl.ds(MARGIN, rows), :]),
        (src.at[:, pl.ds(near, R)], prev.at[pl.ds(0, 2)]),
        (rcv.at[:, pl.ds(near, R)], prev.at[pl.ds(2, 2)]),
        (vel_in.at[pl.ds(near, R)], vel),
    ]
    copies = copies_of(pairs, sems)
    clear(cur, (layers + R) * par)
    band_matrix(matrix)
    inject(cells, traces, 1, delta, base + near)
    wait(copies)
    refs = (cur, prev, vel, delta, matrix, xs)
    step_half(near, refs, scal, wave, depth, 1, base, writer_near(near_part, near_twice))


def last_kernel(
    sy_in, sx_in, hy_in, hx_in, part, twice, halo, vel, near_image, far_a, far_b, src_in, rcv_in,
    image, far_sum, src_last, rcv_last,
    sy, sx, hy, hx, planes, new_near, sems,
):
    del src_in, rcv_in
    scal = (sy, sx, hy, hx)
    near, _ = halves()
    copies = copies_of(zip((sy_in, sx_in, hy_in, hx_in), scal), sems)
    far_sum[...] = far_a[...] + far_b[...]
    wait(copies)

    def write(s, i, new, term):
        new_near[s, i] = new[0]
        new_near[2 + s, i] = new[1]
        image[i] = term + (near_image[i] if s == 0 else image[i])

    finish_near(scal, part, twice, halo, vel, planes, write)
    wait(copies_of([
        (new_near.at[pl.ds(2 * n, 2)], (src_last, rcv_last)[n].at[:, pl.ds(near, R)]) for n in range(2)
    ], sems))


def image_kernel(near_a, near_b, far_a, far_b, out):
    near, far = halves()
    out[pl.ds(near, R)] = near_a[...] + near_b[...]
    out[pl.ds(far, R)] = far_a[...] + far_b[...]


def swap_a(block):
    count = lax.axis_size("slab")
    return lax.ppermute(block, "slab", [(i, i ^ 1) for i in range(count)])


def swap_b(block):
    count = lax.axis_size("slab")
    return lax.ppermute(block, "slab", [(i, ((i + 1) ^ 1) - 1 if 0 < i < count - 1 else count - 1 - i) for i in range(count)])


def swap_shots(block, turn):
    flip = 2 ** (turn + 1) - 1
    count = lax.axis_size("shots")
    return lax.ppermute(block, "shots", [(i, i ^ flip) for i in range(count)])


def shot_rounds(block, turn):
    other = swap_shots(block, turn)
    while 2 ** (turn + 1) < lax.axis_size("shots"):
        turn += 1
        block = block + other
        other = swap_shots(block, turn)
    return block, other


def per_device(
    src_prev, src_cur, rcv_prev, rcv_cur, velocity, wavelet, residual_traces,
    source_depth, source_y, source_x, half_y, half_x, receiver_cell,
):
    layers, rows, cols = velocity.shape
    f32 = jnp.float32
    in_hbm = lambda x: pltpu.with_memory_space_constraint(x, pltpu.HBM)
    src_prev, src_cur, rcv_prev, rcv_cur, velocity, wavelet = (
        in_hbm(x) for x in (src_prev, src_cur, rcv_prev, rcv_cur, velocity, wavelet)
    )
    source_depth, source_y, source_x, half_y, half_x = (
        in_hbm(x) for x in (source_depth, source_y, source_x, half_y, half_x)
    )
    shape = jax.ShapeDtypeStruct
    half4 = shape((4, R, rows, cols), f32)
    half2 = shape((2, R, rows, cols), f32)
    half1 = shape((R, rows, cols), f32)
    packed = shape((4 * R, PACK, cols), f32)
    whole = shape(src_cur.shape, f32)
    dma = lambda n: pltpu.SemaphoreType.DMA((n,))
    planes = pltpu.VMEM((4, R, rows + MARGIN, cols), f32)
    two = pltpu.SMEM(source_y.shape, jnp.int32)
    waves = pltpu.SMEM(wavelet.shape, f32)
    state = lambda deep: [
        pltpu.VMEM((4, layers + 2 * R, rows + 2 * MARGIN, cols), f32),
        pltpu.VMEM((4, deep, rows, cols), f32),
        pltpu.VMEM((deep, rows, cols), f32),
        pltpu.VMEM((2, deep, rows, cols), f32),
        pltpu.VMEM((3 * cols, cols), jnp.bfloat16),
        pltpu.VMEM((4, R, rows, cols), f32),
    ]
    new_half = pltpu.VMEM((4, R, rows, cols), f32)
    scal = (source_y, source_x, half_y, half_x)

    to_b, far_raw = pl.pallas_call(
        pack_kernel,
        out_shape=(packed, half4),
        in_specs=[HBM] * 4,
        out_specs=(VMEM, ANY),
        scratch_shapes=[two, two, planes, dma(10)],
        compiler_params=params(),
        cost_estimate=cost(1 << 20, 1 << 20),
        name="pack_halo",
    )(source_y, source_x, src_cur, rcv_cur)
    from_b = swap_b(to_b)
    halo_a = swap_a(far_raw)

    far_src, far_rcv, far_image, near_part, near_twice, near_vel = pl.pallas_call(
        first_kernel,
        out_shape=(half2, half2, half1, half4, half2, half1),
        in_specs=[HBM] * 10 + [ANY, HBM, VMEM, VMEM],
        out_specs=(VMEM,) * 6,
        scratch_shapes=[two] * 5 + [waves] + state(layers) + [dma(16)],
        compiler_params=params(),
        cost_estimate=cost(1 << 24, 1 << 25),
        name="first_step",
    )(*scal, source_depth, wavelet, src_cur, rcv_cur, src_prev, rcv_prev, halo_a, velocity, receiver_cell, residual_traces)
    halo_src, halo_rcv = swap_a(far_src), swap_a(far_rcv)

    near_cur, near_image, to_b = pl.pallas_call(
        middle_kernel,
        out_shape=(half4, half1, packed),
        in_specs=[HBM] * 4 + [VMEM] * 4,
        out_specs=(VMEM,) * 3,
        scratch_shapes=[two] * 4 + [planes, dma(4)],
        compiler_params=params(),
        cost_estimate=cost(1 << 21, 1 << 26),
        name="first_step_near",
    )(*scal, near_part, near_twice, from_b, near_vel)
    from_b = swap_b(to_b)

    src_last, rcv_last, far_image = pl.pallas_call(
        second_far_kernel,
        out_shape=(whole, whole, half1),
        in_specs=[HBM] * 8 + [ANY] * 5 + [HBM] + [VMEM] * 3,
        out_specs=(HBM, HBM, VMEM),
        scratch_shapes=[two] * 5 + [waves] + state(R) + [new_half, dma(14)],
        compiler_params=params(),
        cost_estimate=cost(1 << 23, 1 << 24),
        name="second_step_far",
    )(*scal, source_depth, wavelet, src_cur, rcv_cur, near_cur, far_src, far_rcv, halo_src, halo_rcv, velocity, receiver_cell, residual_traces, far_image)
    far_other = swap_shots(far_image, 0)

    near_part, near_twice = pl.pallas_call(
        second_near_kernel,
        out_shape=(half4, half2),
        in_specs=[HBM] * 6 + [ANY] * 3 + [HBM] + [VMEM] * 2,
        out_specs=(VMEM, VMEM),
        scratch_shapes=[two] * 3 + [waves] + state(R) + [dma(10)],
        compiler_params=params(),
        cost_estimate=cost(1 << 23, 1 << 24),
        name="second_step_part",
    )(source_y, source_x, source_depth, wavelet, src_cur, rcv_cur, near_cur, far_src, far_rcv, velocity, receiver_cell, residual_traces)

    near_image, far_sum, src_last, rcv_last = pl.pallas_call(
        last_kernel,
        out_shape=(half1, half1, whole, whole),
        in_specs=[HBM] * 4 + [VMEM] * 7 + [HBM] * 2,
        out_specs=(VMEM, VMEM, HBM, HBM),
        scratch_shapes=[two] * 4 + [planes, new_half, dma(4)],
        input_output_aliases={11: 2, 12: 3},
        compiler_params=params(),
        cost_estimate=cost(1 << 21, 1 << 21),
        name="second_step_near",
    )(*scal, near_part, near_twice, from_b, near_vel, near_image, far_image, far_other, src_last, rcv_last)
    near_a, near_b = shot_rounds(near_image, 0)
    far_a, far_b = shot_rounds(far_sum, 1)

    image = pl.pallas_call(
        image_kernel,
        out_shape=shape((layers, rows, cols), f32),
        in_specs=[VMEM] * 4,
        out_specs=VMEM,
        compiler_params=params(),
        cost_estimate=cost(1 << 17, 1 << 20),
        name="image_sum",
    )(near_a, near_b, far_a, far_b)
    return src_last, rcv_last, image


def solution(mesh):
    return jax.shard_map(
        per_device,
        mesh=mesh,
        in_specs=(
            P("shots", "slab", None, None),
            P("shots", "slab", None, None),
            P("shots", "slab", None, None),
            P("shots", "slab", None, None),
            P("slab", None, None),
            P(None, "shots"),
            P(None, "shots", None),
            P("shots"),
            P("shots"),
            P("shots"),
            P("shots"),
            P("shots"),
            P("shots", None),
        ),
        out_specs=(
            P("shots", "slab", None, None),
            P("shots", "slab", None, None),
            P("slab", None, None),
        ),
        check_vma=False,
    )
```

```python
import functools

import jax
import jax.numpy as jnp
from jax import lax
from jax.experimental import pallas as pl
from jax.experimental.pallas import tpu as pltpu
from jax.sharding import PartitionSpec as P

STEPS = 2
COEF = (-205.0 / 72.0, 8.0 / 5.0, -1.0 / 5.0, 8.0 / 315.0, -1.0 / 560.0)
R = 4
HALF_Y, HALF_X = 21, 42
WIN_Y, WIN_X = 2 * HALF_Y + 1, 2 * HALF_X + 1
PACK = 29
REST = WIN_Y - PACK
SCALE = 5040.0
MARGIN = 8

VMEM = pl.BlockSpec(memory_space=pltpu.VMEM)
ANY = pl.BlockSpec(memory_space=pl.ANY)
HBM = pl.BlockSpec(memory_space=pltpu.HBM)


def params(**more):
    return pltpu.CompilerParams(vmem_limit_bytes=24 * 1024 * 1024, **more)


def cost(flops, nbytes):
    return pl.CostEstimate(flops=flops, bytes_accessed=nbytes, transcendentals=0)


def parity():
    return lax.rem(lax.axis_index("slab"), 2)


def halves():
    par = parity()
    return par * R, R - par * R


def lanes(shape):
    return lax.broadcasted_iota(jnp.int32, shape, 1)


def sublanes(shape):
    return lax.broadcasted_iota(jnp.int32, shape, 0)


def band(scal, s, shape):
    sy, sx, hy, hx = (ref[s] for ref in scal)
    return (jnp.abs(sublanes(shape) - sy) <= hy) & (jnp.abs(lanes(shape) - sx) <= hx)


def pack(planes, f, i, row0, col0):
    cols = planes.shape[3]
    main = pltpu.roll(planes[f, i, pl.ds(row0, 32), :], cols - col0, 1)
    left = pltpu.roll(planes[f, i, pl.ds(row0 + PACK, 16), :], lax.rem(WIN_X - col0 + cols, cols), 1)
    right = pltpu.roll(planes[f, i, pl.ds(row0 + PACK - REST + 8, 24), :], lax.rem(HALF_X - col0 + cols, cols), 1)
    left = jnp.concatenate([left, right[8:]], 0)
    right = jnp.concatenate([right[:8], right], 0)
    spare = jnp.where(sublanes(main.shape) < REST, left, right)
    return jnp.where(lanes(main.shape) < WIN_X, main, spare)


def pack_field(planes, f, out, scal, par):
    row0 = scal[0][f % 2] - HALF_Y
    col0 = scal[1][f % 2] - HALF_X
    for d in range(R):
        i = d + par * (R - 1 - 2 * d)
        out[pl.ds((f * R + d) * PACK, PACK), :] = pack(planes, f, i, row0, col0)[:PACK]


def unpack_planes(packed, planes, scal):
    cols = packed.shape[1]
    for f in range(4):
        row0 = scal[0][f % 2] - HALF_Y
        col0 = scal[1][f % 2] - HALF_X
        for e in range(R):
            n = (f * R + e) * PACK
            planes[f, e, pl.ds(row0, PACK), :] = pltpu.roll(packed[pl.ds(n, PACK), :], col0, 1)
            left = pltpu.roll(packed[pl.ds(n, REST), :], lax.rem(col0 + cols - WIN_X, cols), 1)
            right = pltpu.roll(packed[pl.ds(n + REST, REST), :], lax.rem(col0 + cols - HALF_X, cols), 1)
            rest = jnp.where(lanes(left.shape) < col0 + (cols - WIN_X), left, right)
            planes[f, e, pl.ds(row0 + PACK, REST), :] = rest


def copies_of(pairs, sems):
    copies = [pltpu.make_async_copy(a, b, sems.at[n]) for n, (a, b) in enumerate(pairs)]
    for copy in copies:
        copy.start()
    return copies


def wait(copies):
    for copy in copies:
        copy.wait()


def pack_kernel(*refs):
    scal_in, (src, rcv, out), scal, (planes, far_src, far_rcv, sems) = refs[:6], refs[6:9], refs[9:15], refs[15:]
    near, far = halves()
    rows = src.shape[2]
    pairs = list(zip(scal_in, scal))
    for f in range(4):
        ref = (src, rcv)[f // 2].at[f % 2]
        pairs.append((ref.at[pl.ds(near, R)], planes.at[f, :, pl.ds(0, rows), :]))
    for ref, far_ref in ((src, far_src), (rcv, far_rcv)):
        pairs.append((ref.at[:, pl.ds(far, R)], far_ref))
    copies = copies_of(pairs, sems)
    planes[:, :, rows:, :] = jnp.zeros((4, R, MARGIN, planes.shape[3]), jnp.float32)
    wait(copies[:6])
    for f in range(4):
        wait(copies[6 + f : 7 + f])
        pack_field(planes, f, out, scal, parity())
    wait(copies[10:])


def band_matrix(out):
    cols = out.shape[1]
    apart = jnp.abs(sublanes((cols, cols)) - lanes((cols, cols)))
    weights = jnp.zeros((cols, cols), jnp.float32)
    for k in range(1, R + 1):
        weights = jnp.where(apart == k, round(COEF[k] * SCALE) * 1.0, weights)
    for n in range(3):
        out[pl.ds(n * cols, cols)] = weights.astype(jnp.bfloat16)


def x_part(cur, first, matrix, out):
    rows, cols = out.shape[2], out.shape[3]
    for f in range(4):
        rest = cur[f, pl.ds(first + R, R), pl.ds(MARGIN, rows), :].reshape(R * rows, cols)
        parts = []
        for _ in range(3):
            parts.append(rest.astype(jnp.bfloat16))
            rest = rest - parts[-1].astype(jnp.float32)
        total = lax.dot_general(
            jnp.concatenate(parts, 1),
            matrix[...],
            (((1,), (0,)), ((), ())),
            preferred_element_type=jnp.float32,
        )
        out[f] = total.reshape(R, rows, cols)


def laplace(cur, xs, f, i, slot, rows):
    at = lambda layer, row: cur[f, layer, pl.ds(MARGIN + row, rows), :]
    total = 3.0 * COEF[0] * at(slot, 0) + (1.0 / SCALE) * xs[f, i]
    for k in range(1, R + 1):
        side_z = at(slot - k, 0) + at(slot + k, 0)
        side_y = at(slot, -k) + at(slot, k)
        total = total + COEF[k] * (side_z + side_y)
    return total


def inject(cells, traces, first, outs):
    shots, layers, rows, cols = outs[0].shape
    count = cells.shape[1]
    for s in range(shots):
        flat = cells[pl.ds(s, 1), :]
        line = lax.div(flat, cols)
        col = flat - line * cols
        line = line - first * rows
        spot = sublanes((layers * rows, count)) == line
        spot = jnp.where(spot, 1.0, 0.0).astype(jnp.bfloat16)
        here = sublanes((cols, count)) == col
        value = jnp.concatenate(
            [jnp.where(here, traces[step, pl.ds(s, 1), :], 0.0) for step in range(STEPS)], 0
        )
        total = None
        for _ in range(3):
            part = value.astype(jnp.bfloat16)
            value = value - part.astype(jnp.float32)
            term = lax.dot_general(
                spot, part, (((1,), (1,)), ((), ())), preferred_element_type=jnp.float32
            )
            total = term if total is None else total + term
        for step, out in enumerate(outs):
            out[s] = total[:, step * cols : (step + 1) * cols].reshape(layers, rows, cols)


def clear(ref, layers):
    fields, slots, tall, cols = ref.shape
    ref[:, :, :MARGIN, :] = jnp.zeros((fields, slots, MARGIN, cols), jnp.float32)
    ref[:, :, tall - MARGIN :, :] = jnp.zeros((fields, slots, MARGIN, cols), jnp.float32)
    if layers is not None:
        ref[:, pl.ds(layers, R), :, :] = jnp.zeros((fields, R, tall, cols), jnp.float32)


def step_half(first, refs, scal, wave, depth, step, base, write):
    cur, prev, vel, delta, xs = refs
    rows = vel.shape[1]
    for s in range(2):
        spot = (sublanes(vel.shape[1:]) == scal[0][s]) & (lanes(vel.shape[1:]) == scal[1][s])
        here = depth[s] - base

        def layer(i, _):
            p = first + i
            amount = jnp.where(here == p, wave[step, s], 0.0)
            out = []
            for f in (s, 2 + s):
                twice = 2.0 * cur[f, p + R, pl.ds(MARGIN, rows), :] - prev[f, i]
                new = twice + vel[i] * laplace(cur, xs, f, i, p + R, rows)
                if f < 2:
                    new = new + jnp.where(spot, amount, 0.0)
                else:
                    new = new + delta[s, i]
                out.append((twice, new))
            write(s, i, out)
            return 0

        lax.fori_loop(0, R, layer, 0, unroll=True)


def writer_far(scal, new_src, new_rcv, image, before):
    shape = image.shape[1:]

    def write(s, i, out):
        inside = band(scal, s, shape)
        new = [jnp.where(inside, n, 0.0) for _, n in out]
        new_src[s, i] = new[0]
        new_rcv[s, i] = new[1]
        term = (new[0] - out[0][0]) * new[1]
        if s == 0:
            image[i] = term if before is None else term + before[i]
        else:
            image[i] = image[i] + term

    return write


def writer_near(part, twice):
    def write(s, i, out):
        part[s, i] = out[0][1]
        part[2 + s, i] = out[1][1]
        twice[s, i] = out[0][0]

    return write


def first_kernel(
    sy, sx, hy, hx, depth, wave, planes,
    far_src, far_rcv, halo_src, halo_rcv, src_prev, rcv_prev, vel_in, cells, traces,
    src_out, rcv_out, far_image, near_part, near_twice, near_vel, before, vel, later,
    cur, prev, delta, matrix, xs_near, xs_far, sems,
):
    scal = (sy, sx, hy, hx)
    par = parity()
    near, far = halves()
    layers, rows = vel_in.shape[0], vel_in.shape[1]
    base = lax.axis_index("slab") * layers
    inner = pl.ds(MARGIN, rows)
    near_raw = planes.at[:, :, pl.ds(0, rows), :]
    halo = (layers + R) * (1 - par)
    fields = (pl.ds(0, 2), pl.ds(2, 2))
    pairs = [
        (near_raw, cur.at[:, pl.ds(R + near, R), inner, :]),
        (near_raw, before.at[:, pl.ds(near, R)]),
    ]
    for own, other, n in ((far_src, halo_src, 0), (far_rcv, halo_rcv, 1)):
        pairs += [
            (own, cur.at[fields[n], pl.ds(R + far, R), inner, :]),
            (own, before.at[fields[n], pl.ds(far, R)]),
            (other, cur.at[fields[n], pl.ds(halo, R), inner, :]),
        ]
    pairs.append((vel_in, vel))
    for first in (near, far):
        for ref, n in ((src_prev, 0), (rcv_prev, 1)):
            pairs.append((ref.at[:, pl.ds(first, R)], prev.at[fields[n], pl.ds(first, R)]))
    copies = copies_of(pairs, sems)
    clear(cur, (layers + R) * par)
    band_matrix(matrix)
    inject(cells, traces, base, (delta, later))
    wait(copies[:8])
    x_part(cur, near, matrix, xs_near)
    x_part(cur, far, matrix, xs_far)
    wait(copies[8:11])
    has = jnp.where((base == 0) | (lax.axis_index("slab") == lax.axis_size("slab") - 1), 0.0, 1.0)
    near_vel[...] = vel[pl.ds(near, R)] * has

    def half_step(first, xs, write):
        refs = (cur, prev.at[:, pl.ds(first, R)], vel.at[pl.ds(first, R)], delta.at[:, pl.ds(first, R)], xs)
        step_half(first, refs, scal, wave, depth, 0, base, write)

    half_step(near, xs_near, writer_near(near_part, near_twice))
    wait(copies[11:])
    half_step(far, xs_far, writer_far(scal, src_out, rcv_out, far_image, None))


def finish_near(scal, part, twice, halo, vel, planes, write):
    par = parity()
    rows, cols = vel.shape[1], vel.shape[2]
    unpack_planes(halo, planes, scal)
    for s in range(2):
        inside = band(scal, s, (rows, cols))
        for d in range(R):
            i = d + par * (R - 1 - 2 * d)
            new = []
            for f in (s, 2 + s):
                side = COEF[d + 1] * planes[f, 0, pl.ds(0, rows), :]
                for k in range(d + 2, R + 1):
                    side = side + COEF[k] * planes[f, k - d - 1, pl.ds(0, rows), :]
                new.append(jnp.where(inside, part[f, i] + vel[i] * side, 0.0))
            write(s, i, new, (new[0] - twice[s, i]) * new[1])


def middle_kernel(
    sy, sx, hy, hx, part, twice, halo, vel,
    near_out, near_image, packed,
    planes,
):
    scal = (sy, sx, hy, hx)

    def write(s, i, new, term):
        near_out[s, i] = new[0]
        near_out[2 + s, i] = new[1]
        near_image[i] = term if s == 0 else near_image[i] + term

    finish_near(scal, part, twice, halo, vel, planes, write)
    rows = vel.shape[1]
    planes[:, :, pl.ds(0, rows), :] = near_out[...]
    planes[:, :, rows:, :] = jnp.zeros((4, R, MARGIN, planes.shape[3]), jnp.float32)
    for f in range(4):
        pack_field(planes, f, packed, scal, parity())


def second_far_kernel(
    sy, sx, hy, hx, depth, wave,
    before, near_cur, far_src, far_rcv, halo_src, halo_rcv, vel, delta, image_before,
    new_far, image,
    cur, matrix, xs, sems,
):
    scal = (sy, sx, hy, hx)
    par = parity()
    near, far = halves()
    layers, rows = vel.shape[0], vel.shape[1]
    base = lax.axis_index("slab") * layers
    src, rcv = pl.ds(0, 2), pl.ds(2, 2)
    own, halo = pl.ds(R + far, R), pl.ds((layers + R) * (1 - par), R)
    inner = pl.ds(MARGIN, rows)
    copies = copies_of([
        (far_src, cur.at[src, own, inner, :]),
        (far_rcv, cur.at[rcv, own, inner, :]),
        (near_cur, cur.at[:, pl.ds(R + near, R), inner, :]),
        (halo_src, cur.at[src, halo, inner, :]),
        (halo_rcv, cur.at[rcv, halo, inner, :]),
    ], sems)
    clear(cur, None)
    band_matrix(matrix)
    wait(copies)
    x_part(cur, far, matrix, xs)
    refs = (cur, before.at[:, pl.ds(far, R)], vel.at[pl.ds(far, R)], delta.at[:, pl.ds(far, R)], xs)
    write = writer_far(scal, new_far.at[src], new_far.at[rcv], image, image_before)
    step_half(far, refs, scal, wave, depth, 1, base, write)


def second_near_kernel(
    sy, sx, depth, wave,
    before, near_cur, far_src, far_rcv, vel, delta,
    near_part, near_twice,
    cur, matrix, xs, sems,
):
    scal = (sy, sx)
    par = parity()
    near, far = halves()
    layers, rows = vel.shape[0], vel.shape[1]
    base = lax.axis_index("slab") * layers
    inner = pl.ds(MARGIN, rows)
    copies = copies_of([
        (near_cur, cur.at[:, pl.ds(R + near, R), inner, :]),
        (far_src, cur.at[pl.ds(0, 2), pl.ds(R + far, R), inner, :]),
        (far_rcv, cur.at[pl.ds(2, 2), pl.ds(R + far, R), inner, :]),
    ], sems)
    clear(cur, (layers + R) * par)
    band_matrix(matrix)
    wait(copies)
    x_part(cur, near, matrix, xs)
    refs = (cur, before.at[:, pl.ds(near, R)], vel.at[pl.ds(near, R)], delta.at[:, pl.ds(near, R)], xs)
    step_half(near, refs, scal, wave, depth, 1, base, writer_near(near_part, near_twice))


def last_kernel(
    sy, sx, hy, hx, part, twice, halo, vel, near_image, far_a, far_b,
    image, far_sum, new_near,
    planes,
):
    scal = (sy, sx, hy, hx)
    far_sum[...] = far_a[...] + far_b[...]

    def write(s, i, new, term):
        new_near[s, i] = new[0]
        new_near[2 + s, i] = new[1]
        image[i] = term + (near_image[i] if s == 0 else image[i])

    finish_near(scal, part, twice, halo, vel, planes, write)


def write_kernel(new_near, new_far, src_last, rcv_last, sems):
    near, far = halves()
    wait(copies_of([
        (new.at[pl.ds(2 * n, 2)], (src_last, rcv_last)[n].at[:, pl.ds(first, R)])
        for new, first in ((new_near, near), (new_far, far))
        for n in range(2)
    ], sems))


def image_kernel(near_a, near_b, far_a, far_b, out):
    near, far = halves()
    out[pl.ds(near, R)] = near_a[...] + near_b[...]
    out[pl.ds(far, R)] = far_a[...] + far_b[...]


def swap_a(block):
    count = lax.axis_size("slab")
    return lax.ppermute(block, "slab", [(i, i ^ 1) for i in range(count)])


def swap_b(block):
    count = lax.axis_size("slab")
    return lax.ppermute(block, "slab", [(i, ((i + 1) ^ 1) - 1 if 0 < i < count - 1 else count - 1 - i) for i in range(count)])


def swap_shots(block, turn):
    flip = 2 ** (turn + 1) - 1
    count = lax.axis_size("shots")
    return lax.ppermute(block, "shots", [(i, i ^ flip) for i in range(count)])


def shot_rounds(block, turn):
    other = swap_shots(block, turn)
    while 2 ** (turn + 1) < lax.axis_size("shots"):
        turn += 1
        block = block + other
        other = swap_shots(block, turn)
    return block, other


def per_device(
    src_prev, src_cur, rcv_prev, rcv_cur, velocity, wavelet, residual_traces,
    source_depth, source_y, source_x, half_y, half_x, receiver_cell,
):
    layers, rows, cols = velocity.shape
    f32 = jnp.float32
    in_hbm = lambda x: pltpu.with_memory_space_constraint(x, pltpu.HBM)
    src_prev, src_cur, rcv_prev, rcv_cur, velocity = (
        in_hbm(x) for x in (src_prev, src_cur, rcv_prev, rcv_cur, velocity)
    )
    scal_hbm = [
        in_hbm(x) for x in (source_y, source_x, half_y, half_x, source_depth, wavelet)
    ]
    shape = jax.ShapeDtypeStruct
    half4 = shape((4, R, rows, cols), f32)
    half2 = shape((2, R, rows, cols), f32)
    half1 = shape((R, rows, cols), f32)
    packed = shape((4 * R * PACK, cols), f32)
    dma = lambda n: pltpu.SemaphoreType.DMA((n,))
    planes = (4, R, rows + MARGIN, cols)
    state = pltpu.VMEM((4, layers + 2 * R, rows + 2 * MARGIN, cols), f32)
    matrix = pltpu.VMEM((3 * cols, cols), jnp.bfloat16)
    xs = pltpu.VMEM((4, R, rows, cols), f32)

    to_b, *scal, near_raw, far_src, far_rcv = pl.pallas_call(
        pack_kernel,
        out_shape=(packed, *(shape(x.shape, x.dtype) for x in scal_hbm), shape(planes, f32), half2, half2),
        in_specs=[HBM] * 8,
        out_specs=(VMEM,) * 10,
        scratch_shapes=[dma(12)],
        compiler_params=params(),
        cost_estimate=cost(1 << 20, 1 << 20),
        name="pack_halo",
    )(*scal_hbm, src_cur, rcv_cur)
    from_b = swap_b(to_b)
    halo_src, halo_rcv = swap_a(far_src), swap_a(far_rcv)

    far_src, far_rcv, far_image, near_part, near_twice, near_vel, before, vel, later = pl.pallas_call(
        first_kernel,
        out_shape=(half2, half2, half1, half4, half2, half1, shape((4, layers, rows, cols), f32), shape(velocity.shape, f32), shape((2, layers, rows, cols), f32)),
        in_specs=[VMEM] * 9 + [ANY] * 2 + [HBM] * 3 + [VMEM, VMEM],
        out_specs=(VMEM,) * 9,
        scratch_shapes=[state, pltpu.VMEM((4, layers, rows, cols), f32), pltpu.VMEM((2, layers, rows, cols), f32), matrix, xs, xs, dma(13)],
        compiler_params=params(),
        cost_estimate=cost(1 << 24, 1 << 25),
        name="first_step",
    )(*scal, near_raw, far_src, far_rcv, halo_src, halo_rcv, src_prev, rcv_prev, velocity, receiver_cell, residual_traces)
    halo_src, halo_rcv = swap_a(far_src), swap_a(far_rcv)

    near_cur, near_image, to_b = pl.pallas_call(
        middle_kernel,
        out_shape=(half4, half1, packed),
        in_specs=[VMEM] * 8,
        out_specs=(VMEM,) * 3,
        scratch_shapes=[pltpu.VMEM(planes, f32)],
        compiler_params=params(),
        cost_estimate=cost(1 << 21, 1 << 26),
        name="first_step_near",
    )(*scal[:4], near_part, near_twice, from_b, near_vel)
    from_b = swap_b(to_b)

    new_far, far_image = pl.pallas_call(
        second_far_kernel,
        out_shape=(half4, half1),
        in_specs=[VMEM] * 7 + [ANY] * 5 + [VMEM] * 3,
        out_specs=(VMEM, VMEM),
        scratch_shapes=[state, matrix, xs, dma(5)],
        compiler_params=params(),
        cost_estimate=cost(1 << 23, 1 << 24),
        name="second_step_far",
    )(*scal, before, near_cur, far_src, far_rcv, halo_src, halo_rcv, vel, later, far_image)
    far_other = swap_shots(far_image, 0)


    near_part, near_twice = pl.pallas_call(
        second_near_kernel,
        out_shape=(half4, half2),
        in_specs=[VMEM] * 5 + [ANY] * 3 + [VMEM] * 2,
        out_specs=(VMEM, VMEM),
        scratch_shapes=[state, matrix, xs, dma(3)],
        compiler_params=params(),
        cost_estimate=cost(1 << 23, 1 << 24),
        name="second_step_part",
    )(scal[0], scal[1], scal[4], scal[5], before, near_cur, far_src, far_rcv, vel, later)

    near_image, far_image, new_near = pl.pallas_call(
        last_kernel,
        out_shape=(half1, half1, half4),
        in_specs=[VMEM] * 11,
        out_specs=(VMEM,) * 3,
        scratch_shapes=[pltpu.VMEM(planes, f32)],
        compiler_params=params(),
        cost_estimate=cost(1 << 21, 1 << 21),
        name="second_step_near",
    )(*scal[:4], near_part, near_twice, from_b, near_vel, near_image, far_image, far_other)
    near_a, near_b = shot_rounds(near_image, 0)
    far_a, far_b = shot_rounds(far_image, 1)

    src_last, rcv_last = pl.pallas_call(
        write_kernel,
        out_shape=(shape(src_cur.shape, f32),) * 2,
        in_specs=[VMEM, VMEM],
        out_specs=(HBM, HBM),
        scratch_shapes=[dma(4)],
        compiler_params=params(),
        cost_estimate=cost(1 << 10, 1 << 22),
        name="write_fields",
    )(new_near, new_far)

    image = pl.pallas_call(
        image_kernel,
        out_shape=shape((layers, rows, cols), f32),
        in_specs=[VMEM] * 4,
        out_specs=VMEM,
        compiler_params=params(),
        cost_estimate=cost(1 << 17, 1 << 20),
        name="image_sum",
    )(near_a, near_b, far_a, far_b)
    return src_last, rcv_last, image


def solution(mesh):
    return jax.shard_map(
        per_device,
        mesh=mesh,
        in_specs=(
            P("shots", "slab", None, None),
            P("shots", "slab", None, None),
            P("shots", "slab", None, None),
            P("shots", "slab", None, None),
            P("slab", None, None),
            P(None, "shots"),
            P(None, "shots", None),
            P("shots"),
            P("shots"),
            P("shots"),
            P("shots"),
            P("shots"),
            P("shots", None),
        ),
        out_specs=(
            P("shots", "slab", None, None),
            P("shots", "slab", None, None),
            P("slab", None, None),
        ),
        check_vma=False,
    )
```

```python
import functools

import jax
import jax.numpy as jnp
from jax import lax
from jax.experimental import pallas as pl
from jax.experimental.pallas import tpu as pltpu
from jax.sharding import PartitionSpec as P

STEPS = 2
COEF = (-205.0 / 72.0, 8.0 / 5.0, -1.0 / 5.0, 8.0 / 315.0, -1.0 / 560.0)
R = 4
HALF_Y, HALF_X = 21, 42
WIN_Y, WIN_X = 2 * HALF_Y + 1, 2 * HALF_X + 1
PACK = 29
REST = WIN_Y - PACK
SCALE = 5040.0
MARGIN = 8

SPARE = 16
VMEM = pl.BlockSpec(memory_space=pltpu.VMEM)
ANY = pl.BlockSpec(memory_space=pl.ANY)
HBM = pl.BlockSpec(memory_space=pltpu.HBM)


def params(**more):
    return pltpu.CompilerParams(vmem_limit_bytes=24 * 1024 * 1024, **more)


def cost(flops, nbytes):
    return pl.CostEstimate(flops=flops, bytes_accessed=nbytes, transcendentals=0)


def parity():
    return lax.rem(lax.axis_index("slab"), 2)


def halves():
    par = parity()
    return par * R, R - par * R


def lanes(shape):
    return lax.broadcasted_iota(jnp.int32, shape, 1)


def sublanes(shape):
    return lax.broadcasted_iota(jnp.int32, shape, 0)


def band(scal, s, shape):
    sy, sx, hy, hx = (ref[s] for ref in scal)
    return (jnp.abs(sublanes(shape) - sy) <= hy) & (jnp.abs(lanes(shape) - sx) <= hx)


def inside_columns(col0, shape):
    lane = lanes(shape)
    return (lane >= col0) & (lane < col0 + WIN_X)


def pack(planes, f, i, row0, col0):
    main = planes[f, i, pl.ds(row0, 32), :]
    left = pltpu.roll(planes[f, i, pl.ds(row0 + PACK, 16), :], WIN_X, 1)
    right = pltpu.roll(planes[f, i, pl.ds(row0 + PACK - REST + 8, 24), :], HALF_X, 1)
    left = jnp.concatenate([left, right[8:]], 0)
    right = jnp.concatenate([right[:8], right], 0)
    spare = jnp.where(sublanes(main.shape) < REST, left, right)
    return jnp.where(inside_columns(col0, main.shape), main, spare)


def pack_field(planes, f, out, scal, par):
    row0 = scal[0][f % 2] - HALF_Y
    col0 = scal[1][f % 2] - HALF_X
    for d in range(R):
        i = d + par * (R - 1 - 2 * d)
        out[pl.ds((f * R + d) * PACK, PACK), :] = pack(planes, f, i, row0, col0)[:PACK]


def unpack_planes(packed, planes, scal):
    cols = packed.shape[1]
    for f in range(4):
        row0 = scal[0][f % 2] - HALF_Y
        col0 = scal[1][f % 2] - HALF_X
        for e in range(R):
            n = (f * R + e) * PACK
            planes[f, e, pl.ds(row0, PACK), :] = packed[pl.ds(n, PACK), :]
            left = pltpu.roll(packed[pl.ds(n, REST), :], cols - WIN_X, 1)
            right = pltpu.roll(packed[pl.ds(n + REST, REST), :], cols - HALF_X, 1)
            rest = jnp.where(lanes(left.shape) < col0 + (cols - WIN_X), left, right)
            planes[f, e, pl.ds(row0 + PACK, REST), :] = rest


def copies_of(pairs, sems):
    copies = [pltpu.make_async_copy(a, b, sems.at[n]) for n, (a, b) in enumerate(pairs)]
    for copy in copies:
        copy.start()
    return copies


def wait(copies):
    for copy in copies:
        copy.wait()


def pack_kernel(*refs):
    small_in, (src, rcv, out), small, (planes, far_raw, sems) = refs[:8], refs[8:11], refs[11:19], refs[19:]
    near, far = halves()
    rows = src.shape[2]
    pairs = []
    for f in range(4):
        ref = (src, rcv)[f // 2].at[f % 2]
        pairs.append((ref.at[pl.ds(near, R)], planes.at[f, :, pl.ds(0, rows), :]))
    pairs += list(zip(small_in, small))
    for n, ref in enumerate((src, rcv)):
        pairs.append((ref.at[:, pl.ds(far, R)], far_raw.at[pl.ds(2 * n, 2)]))
    copies = copies_of(pairs, sems)
    planes[:, :, rows:, :] = jnp.zeros((4, R, MARGIN, planes.shape[3]), jnp.float32)
    wait(copies[:6])
    for f in range(4):
        pack_field(planes, f, out, small[:2], parity())
    wait(copies[6:])


def band_matrix(out):
    cols = out.shape[1]
    apart = jnp.abs(sublanes((cols, cols)) - lanes((cols, cols)))
    weights = jnp.zeros((cols, cols), jnp.float32)
    for k in range(1, R + 1):
        weights = jnp.where(apart == k, round(COEF[k] * SCALE) * 1.0, weights)
    for n in range(3):
        out[pl.ds(n * cols, cols)] = weights.astype(jnp.bfloat16)


def x_part(cur, first, matrix, out):
    rows, cols = out.shape[2], out.shape[3]
    for f in range(4):
        rest = cur[f, pl.ds(first + R, R), pl.ds(MARGIN, rows), :].reshape(R * rows, cols)
        parts = []
        for _ in range(3):
            parts.append(rest.astype(jnp.bfloat16))
            rest = rest - parts[-1].astype(jnp.float32)
        total = lax.dot_general(
            jnp.concatenate(parts, 1),
            matrix[...],
            (((1,), (0,)), ((), ())),
            preferred_element_type=jnp.float32,
        )
        out[f] = total.reshape(R, rows, cols)


def laplace(cur, xs, f, i, slot, rows):
    at = lambda layer, row: cur[f, layer, pl.ds(MARGIN + row, rows), :]
    total = 3.0 * COEF[0] * at(slot, 0) + (1.0 / SCALE) * xs[f, i]
    for k in range(1, R + 1):
        side_z = at(slot - k, 0) + at(slot + k, 0)
        side_y = at(slot, -k) + at(slot, k)
        total = total + COEF[k] * (side_z + side_y)
    return total


def inject(cells, traces, first, outs):
    shots, layers, rows, cols = outs[0].shape
    count = cells.shape[1]
    for s in range(shots):
        flat = cells[pl.ds(s, 1), :]
        line = lax.div(flat, cols)
        col = flat - line * cols
        line = line - first * rows
        spot = sublanes((layers * rows, count)) == line
        spot = jnp.where(spot, 1.0, 0.0).astype(jnp.bfloat16)
        here = sublanes((cols, count)) == col
        value = jnp.concatenate(
            [jnp.where(here, traces[step, pl.ds(s, 1), :], 0.0) for step in range(STEPS)], 0
        )
        total = None
        for _ in range(3):
            part = value.astype(jnp.bfloat16)
            value = value - part.astype(jnp.float32)
            term = lax.dot_general(
                spot, part, (((1,), (1,)), ((), ())), preferred_element_type=jnp.float32
            )
            total = term if total is None else total + term
        for step, out in enumerate(outs):
            out[s] = total[:, step * cols : (step + 1) * cols].reshape(layers, rows, cols)


def clear(ref, layers):
    fields, slots, tall, cols = ref.shape
    ref[:, :, :MARGIN, :] = jnp.zeros((fields, slots, MARGIN, cols), jnp.float32)
    ref[:, :, tall - MARGIN :, :] = jnp.zeros((fields, slots, MARGIN, cols), jnp.float32)
    if layers is not None:
        ref[:, pl.ds(layers, R), :, :] = jnp.zeros((fields, R, tall, cols), jnp.float32)


def step_half(first, refs, scal, wave, depth, step, base, write):
    cur, prev, vel, delta, xs = refs
    rows = vel.shape[1]
    for s in range(2):
        spot = (sublanes(vel.shape[1:]) == scal[0][s]) & (lanes(vel.shape[1:]) == scal[1][s])
        here = depth[s] - base

        def layer(i, _):
            p = first + i
            amount = jnp.where(here == p, wave[step, s], 0.0)
            out = []
            for f in (s, 2 + s):
                twice = 2.0 * cur[f, p + R, pl.ds(MARGIN, rows), :] - prev[f, i]
                new = twice + vel[i] * laplace(cur, xs, f, i, p + R, rows)
                if f < 2:
                    new = new + jnp.where(spot, amount, 0.0)
                else:
                    new = new + delta[s, i]
                out.append((twice, new))
            write(s, i, out)
            return 0

        lax.fori_loop(0, R, layer, 0, unroll=True)


def writer_far(scal, new_src, new_rcv, image, before):
    shape = image.shape[1:]

    def write(s, i, out):
        inside = band(scal, s, shape)
        new = [jnp.where(inside, n, 0.0) for _, n in out]
        new_src[s, i] = new[0]
        new_rcv[s, i] = new[1]
        term = (new[0] - out[0][0]) * new[1]
        if s == 0:
            image[i] = term if before is None else term + before[i]
        else:
            image[i] = image[i] + term

    return write


def writer_near(part, twice):
    def write(s, i, out):
        part[s, i] = out[0][1]
        part[2 + s, i] = out[1][1]
        twice[s, i] = out[0][0]

    return write


def first_kernel(
    sy, sx, hy, hx, depth, wave, cells, traces, planes, far_raw, halo_raw,
    src_prev, rcv_prev, vel_in,
    src_out, rcv_out, far_image, near_part, near_twice, near_vel, before, vel, later,
    cur, prev, delta, matrix, xs_near, xs_far, sems,
):
    scal = (sy, sx, hy, hx)
    par = parity()
    near, far = halves()
    layers, rows = vel_in.shape[0], vel_in.shape[1]
    base = lax.axis_index("slab") * layers
    inner = pl.ds(MARGIN, rows)
    near_raw = planes.at[:, :, pl.ds(0, rows), :]
    halo = (layers + R) * (1 - par)
    fields = (pl.ds(0, 2), pl.ds(2, 2))
    pairs = [
        (near_raw, cur.at[:, pl.ds(R + near, R), inner, :]),
        (near_raw, before.at[:, pl.ds(near, R)]),
    ]
    pairs += [
        (far_raw, cur.at[:, pl.ds(R + far, R), inner, :]),
        (far_raw, before.at[:, pl.ds(far, R)]),
        (halo_raw, cur.at[:, pl.ds(halo, R), inner, :]),
    ]
    pairs.append((vel_in, vel))
    for first in (near, far):
        for ref, n in ((src_prev, 0), (rcv_prev, 1)):
            pairs.append((ref.at[:, pl.ds(first, R)], prev.at[fields[n], pl.ds(first, R)]))
    copies = copies_of(pairs, sems)
    clear(cur, (layers + R) * par)
    band_matrix(matrix)
    inject(cells, traces, base, (delta, later))
    wait(copies[:5])
    x_part(cur, near, matrix, xs_near)
    x_part(cur, far, matrix, xs_far)
    wait(copies[5:8])
    has = jnp.where((base == 0) | (lax.axis_index("slab") == lax.axis_size("slab") - 1), 0.0, 1.0)
    near_vel[...] = vel[pl.ds(near, R)] * has

    def half_step(first, xs, write):
        refs = (cur, prev.at[:, pl.ds(first, R)], vel.at[pl.ds(first, R)], delta.at[:, pl.ds(first, R)], xs)
        step_half(first, refs, scal, wave, depth, 0, base, write)

    half_step(near, xs_near, writer_near(near_part, near_twice))
    wait(copies[8:])
    half_step(far, xs_far, writer_far(scal, src_out, rcv_out, far_image, None))


def finish_near(scal, part, twice, halo, vel, planes, write):
    par = parity()
    rows, cols = vel.shape[1], vel.shape[2]
    unpack_planes(halo, planes, scal)
    for s in range(2):
        inside = band(scal, s, (rows, cols))
        for d in range(R):
            i = d + par * (R - 1 - 2 * d)
            new = []
            for f in (s, 2 + s):
                side = COEF[d + 1] * planes[f, 0, pl.ds(0, rows), :]
                for k in range(d + 2, R + 1):
                    side = side + COEF[k] * planes[f, k - d - 1, pl.ds(0, rows), :]
                new.append(jnp.where(inside, part[f, i] + vel[i] * side, 0.0))
            write(s, i, new, (new[0] - twice[s, i]) * new[1])


def middle_kernel(
    sy, sx, hy, hx, part, twice, halo, vel,
    near_out, near_image, packed,
    planes,
):
    scal = (sy, sx, hy, hx)
    rows = vel.shape[1]
    near_out[:, :, rows:, :] = jnp.zeros((4, R, MARGIN, planes.shape[3]), jnp.float32)

    def write(s, i, new, term):
        near_out[s, i, pl.ds(0, rows), :] = new[0]
        near_out[2 + s, i, pl.ds(0, rows), :] = new[1]
        near_image[i] = term if s == 0 else near_image[i] + term

    finish_near(scal, part, twice, halo, vel, planes, write)
    for f in range(4):
        pack_field(near_out, f, packed, scal, parity())


def second_far_kernel(
    sy, sx, hy, hx, depth, wave,
    before, near_cur, far_src, far_rcv, halo_src, halo_rcv, vel, delta, image_before,
    new_far, image_out,
    image, cur, matrix, xs, sems,
):
    scal = (sy, sx, hy, hx)
    par = parity()
    near, far = halves()
    layers, rows = vel.shape[0], vel.shape[1]
    base = lax.axis_index("slab") * layers
    src, rcv = pl.ds(0, 2), pl.ds(2, 2)
    own, halo = pl.ds(R + far, R), pl.ds((layers + R) * (1 - par), R)
    inner = pl.ds(MARGIN, rows)
    copies = copies_of([
        (far_src, cur.at[src, own, inner, :]),
        (far_rcv, cur.at[rcv, own, inner, :]),
        (near_cur.at[:, :, pl.ds(0, rows), :], cur.at[:, pl.ds(R + near, R), inner, :]),
        (halo_src, cur.at[src, halo, inner, :]),
        (halo_rcv, cur.at[rcv, halo, inner, :]),
    ], sems)
    clear(cur, None)
    band_matrix(matrix)
    wait(copies)
    x_part(cur, far, matrix, xs)
    refs = (cur, before.at[:, pl.ds(far, R)], vel.at[pl.ds(far, R)], delta.at[:, pl.ds(far, R)], xs)
    write = writer_far(scal, new_far.at[src], new_far.at[rcv], image, image_before)
    step_half(far, refs, scal, wave, depth, 1, base, write)
    used = R * rows
    image_out[:used] = image[...].reshape(used, image.shape[2])
    if image_out.shape[0] > used:
        image_out[used:] = jnp.zeros((image_out.shape[0] - used, image.shape[2]), jnp.float32)


def second_near_kernel(
    sy, sx, depth, wave,
    before, near_cur, far_src, far_rcv, vel, delta,
    near_part, near_twice,
    cur, matrix, xs, sems,
):
    scal = (sy, sx)
    par = parity()
    near, far = halves()
    layers, rows = vel.shape[0], vel.shape[1]
    base = lax.axis_index("slab") * layers
    inner = pl.ds(MARGIN, rows)
    copies = copies_of([
        (near_cur.at[:, :, pl.ds(0, rows), :], cur.at[:, pl.ds(R + near, R), inner, :]),
        (far_src, cur.at[pl.ds(0, 2), pl.ds(R + far, R), inner, :]),
        (far_rcv, cur.at[pl.ds(2, 2), pl.ds(R + far, R), inner, :]),
    ], sems)
    clear(cur, (layers + R) * par)
    band_matrix(matrix)
    wait(copies)
    x_part(cur, near, matrix, xs)
    refs = (cur, before.at[:, pl.ds(near, R)], vel.at[pl.ds(near, R)], delta.at[:, pl.ds(near, R)], xs)
    step_half(near, refs, scal, wave, depth, 1, base, writer_near(near_part, near_twice))


def last_kernel(
    sy, sx, hy, hx, part, twice, halo, vel, near_image,
    image, new_near,
    planes,
):
    scal = (sy, sx, hy, hx)

    def write(s, i, new, term):
        new_near[s, i] = new[0]
        new_near[2 + s, i] = new[1]
        image[i] = term + (near_image[i] if s == 0 else image[i])

    finish_near(scal, part, twice, halo, vel, planes, write)


def write_kernel(new_near, new_far, src_last, rcv_last, sems):
    near, far = halves()
    wait(copies_of([
        (new.at[pl.ds(2 * n, 2)], (src_last, rcv_last)[n].at[:, pl.ds(first, R)])
        for new, first in ((new_near, near), (new_far, far))
        for n in range(2)
    ], sems))


def image_kernel(near_a, near_b, far_a, far_b, out):
    near, far = halves()
    out[pl.ds(near, R)] = near_a[...] + near_b[...]
    used = R * out.shape[1]
    out[pl.ds(far, R)] = (far_a[:used] + far_b[:used]).reshape(R, *out.shape[1:])


def swap_a(block):
    count = lax.axis_size("slab")
    return lax.ppermute(block, "slab", [(i, i ^ 1) for i in range(count)])


def swap_b(block):
    count = lax.axis_size("slab")
    return lax.ppermute(block, "slab", [(i, ((i + 1) ^ 1) - 1 if 0 < i < count - 1 else count - 1 - i) for i in range(count)])


def swap_shots(block, turn):
    flip = 2 ** (turn + 1) - 1
    count = lax.axis_size("shots")
    return lax.ppermute(block, "shots", [(i, i ^ flip) for i in range(count)])


def shot_rounds(block, turns):
    other = swap_shots(block, turns[0])
    turn = turns[1]
    while 2**turn < lax.axis_size("shots"):
        block = block + other
        other = swap_shots(block, turn)
        turn += 1
    return block, other


def per_device(
    src_prev, src_cur, rcv_prev, rcv_cur, velocity, wavelet, residual_traces,
    source_depth, source_y, source_x, half_y, half_x, receiver_cell,
):
    layers, rows, cols = velocity.shape
    f32 = jnp.float32
    in_hbm = lambda x: pltpu.with_memory_space_constraint(x, pltpu.HBM)
    src_prev, src_cur, rcv_prev, rcv_cur, velocity = (
        in_hbm(x) for x in (src_prev, src_cur, rcv_prev, rcv_cur, velocity)
    )
    small_hbm = [
        in_hbm(x)
        for x in (source_y, source_x, half_y, half_x, source_depth, wavelet, receiver_cell, residual_traces)
    ]
    shape = jax.ShapeDtypeStruct
    half4 = shape((4, R, rows, cols), f32)
    half2 = shape((2, R, rows, cols), f32)
    half1 = shape((R, rows, cols), f32)
    far_block = shape((R * rows + SPARE, cols), f32)
    packed = shape((4 * R * PACK, cols), f32)
    dma = lambda n: pltpu.SemaphoreType.DMA((n,))
    planes = (4, R, rows + MARGIN, cols)
    state = pltpu.VMEM((4, layers + 2 * R, rows + 2 * MARGIN, cols), f32)
    matrix = pltpu.VMEM((3 * cols, cols), jnp.bfloat16)
    xs = pltpu.VMEM((4, R, rows, cols), f32)

    to_b, *small, near_raw, far_raw = pl.pallas_call(
        pack_kernel,
        out_shape=(packed, *(shape(x.shape, x.dtype) for x in small_hbm), shape(planes, f32), half4),
        in_specs=[HBM] * 10,
        out_specs=(VMEM,) * 11,
        scratch_shapes=[dma(14)],
        compiler_params=params(),
        cost_estimate=cost(1 << 20, 1 << 20),
        name="pack_halo",
    )(*small_hbm, src_cur, rcv_cur)
    from_b = swap_b(to_b)
    halo_raw = swap_a(far_raw)
    scal = small[:6]

    far_src, far_rcv, far_image, near_part, near_twice, near_vel, before, vel, later = pl.pallas_call(
        first_kernel,
        out_shape=(half2, half2, half1, half4, half2, half1, shape((4, layers, rows, cols), f32), shape(velocity.shape, f32), shape((2, layers, rows, cols), f32)),
        in_specs=[VMEM] * 10 + [ANY] + [HBM] * 3,
        out_specs=(VMEM,) * 9,
        scratch_shapes=[state, pltpu.VMEM((4, layers, rows, cols), f32), pltpu.VMEM((2, layers, rows, cols), f32), matrix, xs, xs, dma(13)],
        compiler_params=params(),
        cost_estimate=cost(1 << 24, 1 << 25),
        name="first_step",
    )(*small, near_raw, far_raw, halo_raw, src_prev, rcv_prev, velocity)
    halo_src, halo_rcv = swap_a(far_src), swap_a(far_rcv)

    near_cur, near_image, to_b = pl.pallas_call(
        middle_kernel,
        out_shape=(shape(planes, f32), half1, packed),
        in_specs=[VMEM] * 8,
        out_specs=(VMEM,) * 3,
        scratch_shapes=[pltpu.VMEM(planes, f32)],
        compiler_params=params(),
        cost_estimate=cost(1 << 21, 1 << 26),
        name="first_step_near",
    )(*scal[:4], near_part, near_twice, from_b, near_vel)
    from_b = swap_b(to_b)

    new_far, far_image = pl.pallas_call(
        second_far_kernel,
        out_shape=(half4, far_block),
        in_specs=[VMEM] * 7 + [ANY] * 5 + [VMEM] * 3,
        out_specs=(VMEM, VMEM),
        scratch_shapes=[pltpu.VMEM((R, rows, cols), f32), state, matrix, xs, dma(5)],
        compiler_params=params(),
        cost_estimate=cost(1 << 23, 1 << 24),
        name="second_step_far",
    )(*scal, before, near_cur, far_src, far_rcv, halo_src, halo_rcv, vel, later, far_image)
    far_other = swap_shots(far_image, 1)


    near_part, near_twice = pl.pallas_call(
        second_near_kernel,
        out_shape=(half4, half2),
        in_specs=[VMEM] * 5 + [ANY] * 3 + [VMEM] * 2,
        out_specs=(VMEM, VMEM),
        scratch_shapes=[state, matrix, xs, dma(3)],
        compiler_params=params(),
        cost_estimate=cost(1 << 23, 1 << 24),
        name="second_step_part",
    )(scal[0], scal[1], scal[4], scal[5], before, near_cur, far_src, far_rcv, vel, later)

    near_image, new_near = pl.pallas_call(
        last_kernel,
        out_shape=(half1, half4),
        in_specs=[VMEM] * 9,
        out_specs=(VMEM,) * 2,
        scratch_shapes=[pltpu.VMEM(planes, f32)],
        compiler_params=params(),
        cost_estimate=cost(1 << 21, 1 << 21),
        name="second_step_near",
    )(*scal[:4], near_part, near_twice, from_b, near_vel, near_image)
    near_other = swap_shots(near_image, 0)
    near_image = near_image + near_other
    far_image = far_image + far_other
    near_a, near_b = shot_rounds(near_image, (1, 2))
    far_a, far_b = shot_rounds(far_image, (0, 2))

    src_last, rcv_last = pl.pallas_call(
        write_kernel,
        out_shape=(shape(src_cur.shape, f32),) * 2,
        in_specs=[VMEM, VMEM],
        out_specs=(HBM, HBM),
        scratch_shapes=[dma(4)],
        compiler_params=params(),
        cost_estimate=cost(1 << 10, 1 << 22),
        name="write_fields",
    )(new_near, new_far)

    image = pl.pallas_call(
        image_kernel,
        out_shape=shape((layers, rows, cols), f32),
        in_specs=[VMEM] * 4,
        out_specs=VMEM,
        compiler_params=params(),
        cost_estimate=cost(1 << 17, 1 << 20),
        name="image_sum",
    )(near_a, near_b, far_a, far_b)
    return src_last, rcv_last, image


def solution(mesh):
    return jax.shard_map(
        per_device,
        mesh=mesh,
        in_specs=(
            P("shots", "slab", None, None),
            P("shots", "slab", None, None),
            P("shots", "slab", None, None),
            P("shots", "slab", None, None),
            P("slab", None, None),
            P(None, "shots"),
            P(None, "shots", None),
            P("shots"),
            P("shots"),
            P("shots"),
            P("shots"),
            P("shots"),
            P("shots", None),
        ),
        out_specs=(
            P("shots", "slab", None, None),
            P("shots", "slab", None, None),
            P("slab", None, None),
        ),
        check_vma=False,
    )
```

```python
import functools

import jax
import jax.numpy as jnp
from jax import lax
from jax.experimental import pallas as pl
from jax.experimental.pallas import tpu as pltpu
from jax.sharding import PartitionSpec as P

STEPS = 2
COEF = (-205.0 / 72.0, 8.0 / 5.0, -1.0 / 5.0, 8.0 / 315.0, -1.0 / 560.0)
R = 4
HALF_Y, HALF_X = 21, 42
WIN_Y, WIN_X = 2 * HALF_Y + 1, 2 * HALF_X + 1
PACK = 29
REST = WIN_Y - PACK
SCALE = 5040.0
MARGIN = 8

SPARE = 16
VMEM = pl.BlockSpec(memory_space=pltpu.VMEM)
ANY = pl.BlockSpec(memory_space=pl.ANY)
HBM = pl.BlockSpec(memory_space=pltpu.HBM)


def params(**more):
    return pltpu.CompilerParams(vmem_limit_bytes=24 * 1024 * 1024, **more)


def cost(flops, nbytes):
    return pl.CostEstimate(flops=flops, bytes_accessed=nbytes, transcendentals=0)


def parity():
    return lax.rem(lax.axis_index("slab"), 2)


def halves():
    par = parity()
    return par * R, R - par * R


def lanes(shape):
    return lax.broadcasted_iota(jnp.int32, shape, 1)


def sublanes(shape):
    return lax.broadcasted_iota(jnp.int32, shape, 0)


def band(scal, s, shape):
    sy, sx, hy, hx = (ref[s] for ref in scal)
    return (jnp.abs(sublanes(shape) - sy) <= hy) & (jnp.abs(lanes(shape) - sx) <= hx)


def inside_columns(col0, shape):
    lane = lanes(shape)
    return (lane >= col0) & (lane < col0 + WIN_X)


def pack(planes, f, i, row0, col0):
    main = planes[f, i, pl.ds(row0, 32), :]
    left = pltpu.roll(planes[f, i, pl.ds(row0 + PACK, 16), :], WIN_X, 1)
    right = pltpu.roll(planes[f, i, pl.ds(row0 + PACK - REST + 8, 24), :], HALF_X, 1)
    left = jnp.concatenate([left, right[8:]], 0)
    right = jnp.concatenate([right[:8], right], 0)
    spare = jnp.where(sublanes(main.shape) < REST, left, right)
    return jnp.where(inside_columns(col0, main.shape), main, spare)


def pack_field(planes, f, out, scal, par):
    row0 = scal[0][f % 2] - HALF_Y
    col0 = scal[1][f % 2] - HALF_X
    for d in range(R):
        i = d + par * (R - 1 - 2 * d)
        out[pl.ds((f * R + d) * PACK, PACK), :] = pack(planes, f, i, row0, col0)[:PACK]


def unpack_planes(packed, planes, scal):
    cols = packed.shape[1]
    for f in range(4):
        row0 = scal[0][f % 2] - HALF_Y
        col0 = scal[1][f % 2] - HALF_X
        for e in range(R):
            n = (f * R + e) * PACK
            planes[f, e, pl.ds(row0, PACK), :] = packed[pl.ds(n, PACK), :]
            left = pltpu.roll(packed[pl.ds(n, REST), :], cols - WIN_X, 1)
            right = pltpu.roll(packed[pl.ds(n + REST, REST), :], cols - HALF_X, 1)
            rest = jnp.where(lanes(left.shape) < col0 + (cols - WIN_X), left, right)
            planes[f, e, pl.ds(row0 + PACK, REST), :] = rest


def copies_of(pairs, sems):
    copies = [pltpu.make_async_copy(a, b, sems.at[n]) for n, (a, b) in enumerate(pairs)]
    for copy in copies:
        copy.start()
    return copies


def wait(copies):
    for copy in copies:
        copy.wait()


def pack_kernel(*refs):
    small_in, (src, rcv, out), small, (planes, far_raw, sems) = refs[:8], refs[8:11], refs[11:19], refs[19:]
    near, far = halves()
    rows = src.shape[2]
    pairs = []
    for f in range(4):
        ref = (src, rcv)[f // 2].at[f % 2]
        pairs.append((ref.at[pl.ds(near, R)], planes.at[f, :, pl.ds(0, rows), :]))
    pairs += list(zip(small_in, small))
    for n, ref in enumerate((src, rcv)):
        pairs.append((ref.at[:, pl.ds(far, R)], far_raw.at[pl.ds(2 * n, 2)]))
    copies = copies_of(pairs, sems)
    planes[:, :, rows:, :] = jnp.zeros((4, R, MARGIN, planes.shape[3]), jnp.float32)
    wait(copies[:6])
    for f in range(4):
        pack_field(planes, f, out, small[:2], parity())
    wait(copies[6:])


def band_matrix(out):
    cols = out.shape[1]
    apart = jnp.abs(sublanes((cols, cols)) - lanes((cols, cols)))
    weights = jnp.zeros((cols, cols), jnp.float32)
    for k in range(1, R + 1):
        weights = jnp.where(apart == k, round(COEF[k] * SCALE) * 1.0, weights)
    for n in range(3):
        out[pl.ds(n * cols, cols)] = weights.astype(jnp.bfloat16)


def x_part(cur, first, matrix, out):
    rows, cols = out.shape[2], out.shape[3]
    for f in range(4):
        rest = cur[f, pl.ds(first + R, R), pl.ds(MARGIN, rows), :].reshape(R * rows, cols)
        parts = []
        for _ in range(3):
            parts.append(rest.astype(jnp.bfloat16))
            rest = rest - parts[-1].astype(jnp.float32)
        total = lax.dot_general(
            jnp.concatenate(parts, 1),
            matrix[...],
            (((1,), (0,)), ((), ())),
            preferred_element_type=jnp.float32,
        )
        out[f] = total.reshape(R, rows, cols)


def laplace(cur, xs, f, i, slot, rows):
    at = lambda layer, row: cur[f, layer, pl.ds(MARGIN + row, rows), :]
    total = 3.0 * COEF[0] * at(slot, 0) + (1.0 / SCALE) * xs[f, i]
    for k in range(1, R + 1):
        side_z = at(slot - k, 0) + at(slot + k, 0)
        side_y = at(slot, -k) + at(slot, k)
        total = total + COEF[k] * (side_z + side_y)
    return total


def inject(cells, traces, first, outs):
    shots, layers, rows, cols = outs[0].shape
    count = cells.shape[1]
    for s in range(shots):
        flat = cells[pl.ds(s, 1), :]
        line = lax.div(flat, cols)
        col = flat - line * cols
        line = line - first * rows
        spot = sublanes((layers * rows, count)) == line
        spot = jnp.where(spot, 1.0, 0.0).astype(jnp.bfloat16)
        here = sublanes((cols, count)) == col
        value = jnp.concatenate(
            [jnp.where(here, traces[step, pl.ds(s, 1), :], 0.0) for step in range(STEPS)], 0
        )
        total = None
        for _ in range(3):
            part = value.astype(jnp.bfloat16)
            value = value - part.astype(jnp.float32)
            term = lax.dot_general(
                spot, part, (((1,), (1,)), ((), ())), preferred_element_type=jnp.float32
            )
            total = term if total is None else total + term
        for step, out in enumerate(outs):
            out[s] = total[:, step * cols : (step + 1) * cols].reshape(layers, rows, cols)


def clear(ref, layers):
    fields, slots, tall, cols = ref.shape
    ref[:, :, :MARGIN, :] = jnp.zeros((fields, slots, MARGIN, cols), jnp.float32)
    ref[:, :, tall - MARGIN :, :] = jnp.zeros((fields, slots, MARGIN, cols), jnp.float32)
    if layers is not None:
        ref[:, pl.ds(layers, R), :, :] = jnp.zeros((fields, R, tall, cols), jnp.float32)


def step_half(first, refs, scal, wave, depth, step, base, write):
    cur, prev, vel, delta, xs = refs
    rows = vel.shape[1]
    for s in range(2):
        spot = (sublanes(vel.shape[1:]) == scal[0][s]) & (lanes(vel.shape[1:]) == scal[1][s])
        here = depth[s] - base

        def layer(i, _):
            p = first + i
            amount = jnp.where(here == p, wave[step, s], 0.0)
            out = []
            for f in (s, 2 + s):
                twice = 2.0 * cur[f, p + R, pl.ds(MARGIN, rows), :] - prev[f, i]
                new = twice + vel[i] * laplace(cur, xs, f, i, p + R, rows)
                if f < 2:
                    new = new + jnp.where(spot, amount, 0.0)
                else:
                    new = new + delta[s, i]
                out.append((twice, new))
            write(s, i, out)
            return 0

        lax.fori_loop(0, R, layer, 0, unroll=True)


def writer_far(scal, new_src, new_rcv, image, before):
    shape = image.shape[1:]

    def write(s, i, out):
        inside = band(scal, s, shape)
        new = [jnp.where(inside, n, 0.0) for _, n in out]
        new_src[s, i] = new[0]
        new_rcv[s, i] = new[1]
        term = (new[0] - out[0][0]) * new[1]
        if s == 0:
            image[i] = term if before is None else term + before[i]
        else:
            image[i] = image[i] + term

    return write


def writer_near(part, twice):
    def write(s, i, out):
        part[s, i] = out[0][1]
        part[2 + s, i] = out[1][1]
        twice[s, i] = out[0][0]

    return write


def first_kernel(
    sy, sx, hy, hx, depth, wave, cells, traces, planes, far_raw, halo_raw,
    src_prev, rcv_prev, vel_in,
    src_out, rcv_out, far_image, near_part, near_twice, near_vel, before, vel, later,
    cur, prev, delta, matrix, xs_near, xs_far, sems,
):
    scal = (sy, sx, hy, hx)
    par = parity()
    near, far = halves()
    layers, rows = vel_in.shape[0], vel_in.shape[1]
    base = lax.axis_index("slab") * layers
    inner = pl.ds(MARGIN, rows)
    near_raw = planes.at[:, :, pl.ds(0, rows), :]
    halo = (layers + R) * (1 - par)
    fields = (pl.ds(0, 2), pl.ds(2, 2))
    pairs = [
        (near_raw, cur.at[:, pl.ds(R + near, R), inner, :]),
        (near_raw, before.at[:, pl.ds(near, R)]),
    ]
    pairs += [
        (far_raw, cur.at[:, pl.ds(R + far, R), inner, :]),
        (far_raw, before.at[:, pl.ds(far, R)]),
        (halo_raw, cur.at[:, pl.ds(halo, R), inner, :]),
    ]
    pairs.append((vel_in, vel))
    for first in (near, far):
        for ref, n in ((src_prev, 0), (rcv_prev, 1)):
            pairs.append((ref.at[:, pl.ds(first, R)], prev.at[fields[n], pl.ds(first, R)]))
    copies = copies_of(pairs, sems)
    clear(cur, (layers + R) * par)
    band_matrix(matrix)
    inject(cells, traces, base, (delta, later))
    wait(copies[:5])
    x_part(cur, near, matrix, xs_near)
    x_part(cur, far, matrix, xs_far)
    wait(copies[5:8])
    has = jnp.where((base == 0) | (lax.axis_index("slab") == lax.axis_size("slab") - 1), 0.0, 1.0)
    near_vel[...] = vel[pl.ds(near, R)] * has

    def half_step(first, xs, write):
        refs = (cur, prev.at[:, pl.ds(first, R)], vel.at[pl.ds(first, R)], delta.at[:, pl.ds(first, R)], xs)
        step_half(first, refs, scal, wave, depth, 0, base, write)

    half_step(near, xs_near, writer_near(near_part, near_twice))
    wait(copies[8:])
    half_step(far, xs_far, writer_far(scal, src_out, rcv_out, far_image, None))


def finish_near(scal, part, twice, halo, vel, planes, write):
    par = parity()
    rows, cols = vel.shape[1], vel.shape[2]
    unpack_planes(halo, planes, scal)
    for s in range(2):
        inside = band(scal, s, (rows, cols))
        for d in range(R):
            i = d + par * (R - 1 - 2 * d)
            new = []
            for f in (s, 2 + s):
                side = COEF[d + 1] * planes[f, 0, pl.ds(0, rows), :]
                for k in range(d + 2, R + 1):
                    side = side + COEF[k] * planes[f, k - d - 1, pl.ds(0, rows), :]
                new.append(jnp.where(inside, part[f, i] + vel[i] * side, 0.0))
            write(s, i, new, (new[0] - twice[s, i]) * new[1])


def middle_kernel(
    sy, sx, hy, hx, part, twice, halo, vel,
    near_out, near_image, packed,
    planes,
):
    scal = (sy, sx, hy, hx)
    rows = vel.shape[1]
    near_out[:, :, rows:, :] = jnp.zeros((4, R, MARGIN, planes.shape[3]), jnp.float32)

    def write(s, i, new, term):
        near_out[s, i, pl.ds(0, rows), :] = new[0]
        near_out[2 + s, i, pl.ds(0, rows), :] = new[1]
        near_image[i] = term if s == 0 else near_image[i] + term

    finish_near(scal, part, twice, halo, vel, planes, write)
    for f in range(4):
        pack_field(near_out, f, packed, scal, parity())


def second_far_kernel(
    sy, sx, hy, hx, depth, wave,
    before, near_cur, far_src, far_rcv, halo_src, halo_rcv, vel, delta, image_before,
    new_far, image_out,
    image, cur, matrix, xs, sems,
):
    scal = (sy, sx, hy, hx)
    par = parity()
    near, far = halves()
    layers, rows = vel.shape[0], vel.shape[1]
    base = lax.axis_index("slab") * layers
    src, rcv = pl.ds(0, 2), pl.ds(2, 2)
    own, halo = pl.ds(R + far, R), pl.ds((layers + R) * (1 - par), R)
    inner = pl.ds(MARGIN, rows)
    copies = copies_of([
        (far_src, cur.at[src, own, inner, :]),
        (far_rcv, cur.at[rcv, own, inner, :]),
        (near_cur.at[:, :, pl.ds(0, rows), :], cur.at[:, pl.ds(R + near, R), inner, :]),
        (halo_src, cur.at[src, halo, inner, :]),
        (halo_rcv, cur.at[rcv, halo, inner, :]),
    ], sems)
    clear(cur, None)
    band_matrix(matrix)
    wait(copies)
    x_part(cur, far, matrix, xs)
    refs = (cur, before.at[:, pl.ds(far, R)], vel.at[pl.ds(far, R)], delta.at[:, pl.ds(far, R)], xs)
    write = writer_far(scal, new_far.at[src], new_far.at[rcv], image, image_before)
    step_half(far, refs, scal, wave, depth, 1, base, write)
    used = R * rows
    image_out[:used] = image[...].reshape(used, image.shape[2])
    if image_out.shape[0] > used:
        image_out[used:] = jnp.zeros((image_out.shape[0] - used, image.shape[2]), jnp.float32)


def second_near_kernel(
    sy, sx, depth, wave,
    before, near_cur, far_src, far_rcv, vel, delta,
    near_part, near_twice,
    cur, matrix, xs, sems,
):
    scal = (sy, sx)
    par = parity()
    near, far = halves()
    layers, rows = vel.shape[0], vel.shape[1]
    base = lax.axis_index("slab") * layers
    inner = pl.ds(MARGIN, rows)
    copies = copies_of([
        (near_cur.at[:, :, pl.ds(0, rows), :], cur.at[:, pl.ds(R + near, R), inner, :]),
        (far_src, cur.at[pl.ds(0, 2), pl.ds(R + far, R), inner, :]),
        (far_rcv, cur.at[pl.ds(2, 2), pl.ds(R + far, R), inner, :]),
    ], sems)
    clear(cur, (layers + R) * par)
    band_matrix(matrix)
    wait(copies)
    x_part(cur, near, matrix, xs)
    refs = (cur, before.at[:, pl.ds(near, R)], vel.at[pl.ds(near, R)], delta.at[:, pl.ds(near, R)], xs)
    step_half(near, refs, scal, wave, depth, 1, base, writer_near(near_part, near_twice))


def last_kernel(
    sy, sx, hy, hx, part, twice, halo, vel, near_image,
    image, new_near,
    planes,
):
    scal = (sy, sx, hy, hx)

    def write(s, i, new, term):
        new_near[s, i] = new[0]
        new_near[2 + s, i] = new[1]
        image[i] = term + (near_image[i] if s == 0 else image[i])

    finish_near(scal, part, twice, halo, vel, planes, write)


def write_kernel(new_near, new_far, src_last, rcv_last, sems):
    near, far = halves()
    wait(copies_of([
        (new.at[pl.ds(2 * n, 2)], (src_last, rcv_last)[n].at[:, pl.ds(first, R)])
        for new, first in ((new_near, near), (new_far, far))
        for n in range(2)
    ], sems))


def image_kernel(near_a, near_b, far_a, far_b, out):
    near, far = halves()
    out[pl.ds(near, R)] = near_a[...] + near_b[...]
    used = R * out.shape[1]
    out[pl.ds(far, R)] = (far_a[:used] + far_b[:used]).reshape(R, *out.shape[1:])


def swap_a(block):
    count = lax.axis_size("slab")
    return lax.ppermute(block, "slab", [(i, i ^ 1) for i in range(count)])


def swap_b(block):
    count, groups = lax.axis_size("slab"), lax.axis_size("shots")
    pairs = []
    for i in range(count):
        for g in range(groups):
            to = (i, g ^ 1) if i in (0, count - 1) else (((i + 1) ^ 1) - 1, g)
            pairs.append((i * groups + g, to[0] * groups + to[1]))
    return lax.ppermute(block, ("slab", "shots"), pairs)


def swap_shots(block, turn):
    flip = 2 ** (turn + 1) - 1
    count = lax.axis_size("shots")
    return lax.ppermute(block, "shots", [(i, i ^ flip) for i in range(count)])


def shot_rounds(block, turns):
    other = swap_shots(block, turns[0])
    turn = turns[1]
    while 2**turn < lax.axis_size("shots"):
        block = block + other
        other = swap_shots(block, turn)
        turn += 1
    return block, other


def per_device(
    src_prev, src_cur, rcv_prev, rcv_cur, velocity, wavelet, residual_traces,
    source_depth, source_y, source_x, half_y, half_x, receiver_cell,
):
    layers, rows, cols = velocity.shape
    f32 = jnp.float32
    in_hbm = lambda x: pltpu.with_memory_space_constraint(x, pltpu.HBM)
    src_prev, src_cur, rcv_prev, rcv_cur, velocity = (
        in_hbm(x) for x in (src_prev, src_cur, rcv_prev, rcv_cur, velocity)
    )
    small_hbm = [
        in_hbm(x)
        for x in (source_y, source_x, half_y, half_x, source_depth, wavelet, receiver_cell, residual_traces)
    ]
    shape = jax.ShapeDtypeStruct
    half4 = shape((4, R, rows, cols), f32)
    half2 = shape((2, R, rows, cols), f32)
    half1 = shape((R, rows, cols), f32)
    far_block = shape((R * rows + SPARE, cols), f32)
    packed = shape((4 * R * PACK, cols), f32)
    dma = lambda n: pltpu.SemaphoreType.DMA((n,))
    planes = (4, R, rows + MARGIN, cols)
    state = pltpu.VMEM((4, layers + 2 * R, rows + 2 * MARGIN, cols), f32)
    matrix = pltpu.VMEM((3 * cols, cols), jnp.bfloat16)
    xs = pltpu.VMEM((4, R, rows, cols), f32)

    to_b, *small, near_raw, far_raw = pl.pallas_call(
        pack_kernel,
        out_shape=(packed, *(shape(x.shape, x.dtype) for x in small_hbm), shape(planes, f32), half4),
        in_specs=[HBM] * 10,
        out_specs=(VMEM,) * 11,
        scratch_shapes=[dma(14)],
        compiler_params=params(),
        cost_estimate=cost(1 << 20, 1 << 20),
        name="pack_halo",
    )(*small_hbm, src_cur, rcv_cur)
    from_b = swap_b(to_b)
    halo_raw = swap_a(far_raw)
    scal = small[:6]

    far_src, far_rcv, far_image, near_part, near_twice, near_vel, before, vel, later = pl.pallas_call(
        first_kernel,
        out_shape=(half2, half2, half1, half4, half2, half1, shape((4, layers, rows, cols), f32), shape(velocity.shape, f32), shape((2, layers, rows, cols), f32)),
        in_specs=[VMEM] * 10 + [ANY] + [HBM] * 3,
        out_specs=(VMEM,) * 9,
        scratch_shapes=[state, pltpu.VMEM((4, layers, rows, cols), f32), pltpu.VMEM((2, layers, rows, cols), f32), matrix, xs, xs, dma(13)],
        compiler_params=params(),
        cost_estimate=cost(1 << 24, 1 << 25),
        name="first_step",
    )(*small, near_raw, far_raw, halo_raw, src_prev, rcv_prev, velocity)
    halo_src, halo_rcv = swap_a(far_src), swap_a(far_rcv)

    near_cur, near_image, to_b = pl.pallas_call(
        middle_kernel,
        out_shape=(shape(planes, f32), half1, packed),
        in_specs=[VMEM] * 8,
        out_specs=(VMEM,) * 3,
        scratch_shapes=[pltpu.VMEM(planes, f32)],
        compiler_params=params(),
        cost_estimate=cost(1 << 21, 1 << 26),
        name="first_step_near",
    )(*scal[:4], near_part, near_twice, from_b, near_vel)
    from_b = swap_b(to_b)

    new_far, far_image = pl.pallas_call(
        second_far_kernel,
        out_shape=(half4, far_block),
        in_specs=[VMEM] * 7 + [ANY] * 5 + [VMEM] * 3,
        out_specs=(VMEM, VMEM),
        scratch_shapes=[pltpu.VMEM((R, rows, cols), f32), state, matrix, xs, dma(5)],
        compiler_params=params(),
        cost_estimate=cost(1 << 23, 1 << 24),
        name="second_step_far",
    )(*scal, before, near_cur, far_src, far_rcv, halo_src, halo_rcv, vel, later, far_image)
    far_other = swap_shots(far_image, 1)


    near_part, near_twice = pl.pallas_call(
        second_near_kernel,
        out_shape=(half4, half2),
        in_specs=[VMEM] * 5 + [ANY] * 3 + [VMEM] * 2,
        out_specs=(VMEM, VMEM),
        scratch_shapes=[state, matrix, xs, dma(3)],
        compiler_params=params(),
        cost_estimate=cost(1 << 23, 1 << 24),
        name="second_step_part",
    )(scal[0], scal[1], scal[4], scal[5], before, near_cur, far_src, far_rcv, vel, later)

    near_image, new_near = pl.pallas_call(
        last_kernel,
        out_shape=(half1, half4),
        in_specs=[VMEM] * 9,
        out_specs=(VMEM,) * 2,
        scratch_shapes=[pltpu.VMEM(planes, f32)],
        compiler_params=params(),
        cost_estimate=cost(1 << 21, 1 << 21),
        name="second_step_near",
    )(*scal[:4], near_part, near_twice, from_b, near_vel, near_image)
    near_other = swap_shots(near_image, 0)
    near_image = near_image + near_other
    far_image = far_image + far_other
    near_a, near_b = shot_rounds(near_image, (1, 2))
    far_a, far_b = shot_rounds(far_image, (0, 2))

    src_last, rcv_last = pl.pallas_call(
        write_kernel,
        out_shape=(shape(src_cur.shape, f32),) * 2,
        in_specs=[VMEM, VMEM],
        out_specs=(HBM, HBM),
        scratch_shapes=[dma(4)],
        compiler_params=params(),
        cost_estimate=cost(1 << 10, 1 << 22),
        name="write_fields",
    )(new_near, new_far)

    image = pl.pallas_call(
        image_kernel,
        out_shape=shape((layers, rows, cols), f32),
        in_specs=[VMEM] * 4,
        out_specs=VMEM,
        compiler_params=params(),
        cost_estimate=cost(1 << 17, 1 << 20),
        name="image_sum",
    )(near_a, near_b, far_a, far_b)
    return src_last, rcv_last, image


def solution(mesh):
    return jax.shard_map(
        per_device,
        mesh=mesh,
        in_specs=(
            P("shots", "slab", None, None),
            P("shots", "slab", None, None),
            P("shots", "slab", None, None),
            P("shots", "slab", None, None),
            P("slab", None, None),
            P(None, "shots"),
            P(None, "shots", None),
            P("shots"),
            P("shots"),
            P("shots"),
            P("shots"),
            P("shots"),
            P("shots", None),
        ),
        out_specs=(
            P("shots", "slab", None, None),
            P("shots", "slab", None, None),
            P("slab", None, None),
        ),
        check_vma=False,
    )
```

```python
import functools

import jax
import jax.numpy as jnp
from jax import lax
from jax.experimental import pallas as pl
from jax.experimental.pallas import tpu as pltpu
from jax.sharding import PartitionSpec as P

STEPS = 2
COEF = (-205.0 / 72.0, 8.0 / 5.0, -1.0 / 5.0, 8.0 / 315.0, -1.0 / 560.0)
R = 4
HALF_Y, HALF_X = 21, 42
WIN_Y, WIN_X = 2 * HALF_Y + 1, 2 * HALF_X + 1
PACK = 29
TAIL = 8
REST = WIN_Y - PACK
SCALE = 5040.0
MARGIN = 8

SPARE = 16
VMEM = pl.BlockSpec(memory_space=pltpu.VMEM)
ANY = pl.BlockSpec(memory_space=pl.ANY)
HBM = pl.BlockSpec(memory_space=pltpu.HBM)


def params(**more):
    return pltpu.CompilerParams(vmem_limit_bytes=24 * 1024 * 1024, **more)


def cost(flops, nbytes):
    return pl.CostEstimate(flops=flops, bytes_accessed=nbytes, transcendentals=0)


def parity():
    return lax.rem(lax.axis_index("slab"), 2)


def halves():
    par = parity()
    return par * R, R - par * R


def lanes(shape):
    return lax.broadcasted_iota(jnp.int32, shape, 1)


def sublanes(shape):
    return lax.broadcasted_iota(jnp.int32, shape, 0)


def band(scal, s, shape):
    sy, sx, hy, hx = (ref[s] for ref in scal)
    return (jnp.abs(sublanes(shape) - sy) <= hy) & (jnp.abs(lanes(shape) - sx) <= hx)


def inside_columns(col0, shape):
    lane = lanes(shape)
    return (lane >= col0) & (lane < col0 + WIN_X)


def pack(planes, f, i, row0, col0):
    main = planes[f, i, pl.ds(row0, 32), :]
    left = pltpu.roll(planes[f, i, pl.ds(row0 + PACK, 16), :], WIN_X, 1)
    right = pltpu.roll(planes[f, i, pl.ds(row0 + PACK - REST + 8, 24), :], HALF_X, 1)
    left = jnp.concatenate([left, right[8:]], 0)
    right = jnp.concatenate([right[:8], right], 0)
    spare = jnp.where(sublanes(main.shape) < REST, left, right)
    return jnp.where(inside_columns(col0, main.shape), main, spare)


def pack_field(planes, f, out, scal, par):
    if f == 0:
        out[4 * R * PACK :] = jnp.zeros((TAIL, out.shape[1]), jnp.float32)
    row0 = scal[0][f % 2] - HALF_Y
    col0 = scal[1][f % 2] - HALF_X
    for d in range(R):
        i = d + par * (R - 1 - 2 * d)
        out[pl.ds((f * R + d) * PACK, PACK), :] = pack(planes, f, i, row0, col0)[:PACK]


def unpack_planes(packed, planes, scal):
    cols = packed.shape[1]
    for f in range(4):
        row0 = scal[0][f % 2] - HALF_Y
        col0 = scal[1][f % 2] - HALF_X
        for e in range(R):
            n = (f * R + e) * PACK
            planes[f, e, pl.ds(row0, PACK), :] = packed[pl.ds(n, PACK), :]
            left = pltpu.roll(packed[pl.ds(n, REST), :], cols - WIN_X, 1)
            right = pltpu.roll(packed[pl.ds(n + REST, REST), :], cols - HALF_X, 1)
            rest = jnp.where(lanes(left.shape) < col0 + (cols - WIN_X), left, right)
            planes[f, e, pl.ds(row0 + PACK, REST), :] = rest


def copies_of(pairs, sems):
    copies = [pltpu.make_async_copy(a, b, sems.at[n]) for n, (a, b) in enumerate(pairs)]
    for copy in copies:
        copy.start()
    return copies


def wait(copies):
    for copy in copies:
        copy.wait()


def pack_kernel(*refs):
    small_in, (src, rcv, out), small, (planes, far_raw, sems) = refs[:8], refs[8:11], refs[11:19], refs[19:]
    near, far = halves()
    rows = src.shape[2]
    pairs = []
    for f in range(4):
        ref = (src, rcv)[f // 2].at[f % 2]
        pairs.append((ref.at[pl.ds(near, R)], planes.at[f, :, pl.ds(0, rows), :]))
    pairs += list(zip(small_in, small))
    for n, ref in enumerate((src, rcv)):
        pairs.append((ref.at[:, pl.ds(far, R)], far_raw.at[pl.ds(2 * n, 2)]))
    copies = copies_of(pairs, sems)
    planes[:, :, rows:, :] = jnp.zeros((4, R, MARGIN, planes.shape[3]), jnp.float32)
    wait(copies[:6])
    for f in range(4):
        pack_field(planes, f, out, small[:2], parity())
    wait(copies[6:])


def band_matrix(out):
    cols = out.shape[1]
    apart = jnp.abs(sublanes((cols, cols)) - lanes((cols, cols)))
    weights = jnp.zeros((cols, cols), jnp.float32)
    for k in range(1, R + 1):
        weights = jnp.where(apart == k, round(COEF[k] * SCALE) * 1.0, weights)
    for n in range(3):
        out[pl.ds(n * cols, cols)] = weights.astype(jnp.bfloat16)


def x_part(cur, first, matrix, out):
    rows, cols = out.shape[2], out.shape[3]
    for f in range(4):
        rest = cur[f, pl.ds(first + R, R), pl.ds(MARGIN, rows), :].reshape(R * rows, cols)
        parts = []
        for _ in range(3):
            parts.append(rest.astype(jnp.bfloat16))
            rest = rest - parts[-1].astype(jnp.float32)
        total = lax.dot_general(
            jnp.concatenate(parts, 1),
            matrix[...],
            (((1,), (0,)), ((), ())),
            preferred_element_type=jnp.float32,
        )
        out[f] = total.reshape(R, rows, cols)


def laplace(cur, xs, f, i, slot, rows):
    at = lambda layer, row: cur[f, layer, pl.ds(MARGIN + row, rows), :]
    total = 3.0 * COEF[0] * at(slot, 0) + (1.0 / SCALE) * xs[f, i]
    for k in range(1, R + 1):
        side_z = at(slot - k, 0) + at(slot + k, 0)
        side_y = at(slot, -k) + at(slot, k)
        total = total + COEF[k] * (side_z + side_y)
    return total


def inject(cells, traces, first, outs):
    shots, layers, rows, cols = outs[0].shape
    count = cells.shape[1]
    for s in range(shots):
        flat = cells[pl.ds(s, 1), :]
        line = lax.div(flat, cols)
        col = flat - line * cols
        line = line - first * rows
        spot = sublanes((layers * rows, count)) == line
        spot = jnp.where(spot, 1.0, 0.0).astype(jnp.bfloat16)
        here = sublanes((cols, count)) == col
        value = jnp.concatenate(
            [jnp.where(here, traces[step, pl.ds(s, 1), :], 0.0) for step in range(STEPS)], 0
        )
        total = None
        for _ in range(3):
            part = value.astype(jnp.bfloat16)
            value = value - part.astype(jnp.float32)
            term = lax.dot_general(
                spot, part, (((1,), (1,)), ((), ())), preferred_element_type=jnp.float32
            )
            total = term if total is None else total + term
        for step, out in enumerate(outs):
            out[s] = total[:, step * cols : (step + 1) * cols].reshape(layers, rows, cols)


def clear(ref, layers):
    fields, slots, tall, cols = ref.shape
    ref[:, :, :MARGIN, :] = jnp.zeros((fields, slots, MARGIN, cols), jnp.float32)
    ref[:, :, tall - MARGIN :, :] = jnp.zeros((fields, slots, MARGIN, cols), jnp.float32)
    if layers is not None:
        ref[:, pl.ds(layers, R), :, :] = jnp.zeros((fields, R, tall, cols), jnp.float32)


def step_half(first, refs, scal, wave, depth, step, base, write):
    cur, prev, vel, delta, xs = refs
    rows = vel.shape[1]
    for s in range(2):
        spot = (sublanes(vel.shape[1:]) == scal[0][s]) & (lanes(vel.shape[1:]) == scal[1][s])
        here = depth[s] - base

        def layer(i, _):
            p = first + i
            amount = jnp.where(here == p, wave[step, s], 0.0)
            out = []
            for f in (s, 2 + s):
                twice = 2.0 * cur[f, p + R, pl.ds(MARGIN, rows), :] - prev[f, i]
                new = twice + vel[i] * laplace(cur, xs, f, i, p + R, rows)
                if f < 2:
                    new = new + jnp.where(spot, amount, 0.0)
                else:
                    new = new + delta[s, i]
                out.append((twice, new))
            write(s, i, out)
            return 0

        lax.fori_loop(0, R, layer, 0, unroll=True)


def writer_far(scal, new_src, new_rcv, image, before):
    shape = image.shape[1:]

    def write(s, i, out):
        inside = band(scal, s, shape)
        new = [jnp.where(inside, n, 0.0) for _, n in out]
        new_src[s, i] = new[0]
        new_rcv[s, i] = new[1]
        term = (new[0] - out[0][0]) * new[1]
        if s == 0:
            image[i] = term if before is None else term + before[i]
        else:
            image[i] = image[i] + term

    return write


def writer_near(part, twice):
    def write(s, i, out):
        part[s, i] = out[0][1]
        part[2 + s, i] = out[1][1]
        twice[s, i] = out[0][0]

    return write


def first_kernel(
    sy, sx, hy, hx, depth, wave, cells, traces, planes, far_raw, halo_raw,
    src_prev, rcv_prev, vel_in,
    src_out, rcv_out, far_image, near_part, near_twice, near_vel, before, vel, later,
    cur, prev, delta, matrix, xs_near, xs_far, sems,
):
    scal = (sy, sx, hy, hx)
    par = parity()
    near, far = halves()
    layers, rows = vel_in.shape[0], vel_in.shape[1]
    base = lax.axis_index("slab") * layers
    inner = pl.ds(MARGIN, rows)
    near_raw = planes.at[:, :, pl.ds(0, rows), :]
    halo = (layers + R) * (1 - par)
    fields = (pl.ds(0, 2), pl.ds(2, 2))
    pairs = [
        (near_raw, cur.at[:, pl.ds(R + near, R), inner, :]),
        (near_raw, before.at[:, pl.ds(near, R)]),
    ]
    pairs += [
        (far_raw, cur.at[:, pl.ds(R + far, R), inner, :]),
        (far_raw, before.at[:, pl.ds(far, R)]),
        (halo_raw, cur.at[:, pl.ds(halo, R), inner, :]),
    ]
    pairs.append((vel_in, vel))
    for first in (near, far):
        for ref, n in ((src_prev, 0), (rcv_prev, 1)):
            pairs.append((ref.at[:, pl.ds(first, R)], prev.at[fields[n], pl.ds(first, R)]))
    copies = copies_of(pairs, sems)
    clear(cur, (layers + R) * par)
    band_matrix(matrix)
    inject(cells, traces, base, (delta, later))
    wait(copies[:5])
    x_part(cur, near, matrix, xs_near)
    x_part(cur, far, matrix, xs_far)
    wait(copies[5:8])
    has = jnp.where((base == 0) | (lax.axis_index("slab") == lax.axis_size("slab") - 1), 0.0, 1.0)
    near_vel[...] = vel[pl.ds(near, R)] * has

    def half_step(first, xs, write):
        refs = (cur, prev.at[:, pl.ds(first, R)], vel.at[pl.ds(first, R)], delta.at[:, pl.ds(first, R)], xs)
        step_half(first, refs, scal, wave, depth, 0, base, write)

    half_step(near, xs_near, writer_near(near_part, near_twice))
    wait(copies[8:])
    half_step(far, xs_far, writer_far(scal, src_out, rcv_out, far_image, None))


def finish_near(scal, part, twice, halo, vel, planes, write):
    par = parity()
    rows, cols = vel.shape[1], vel.shape[2]
    unpack_planes(halo, planes, scal)
    for s in range(2):
        inside = band(scal, s, (rows, cols))
        for d in range(R):
            i = d + par * (R - 1 - 2 * d)
            new = []
            for f in (s, 2 + s):
                side = COEF[d + 1] * planes[f, 0, pl.ds(0, rows), :]
                for k in range(d + 2, R + 1):
                    side = side + COEF[k] * planes[f, k - d - 1, pl.ds(0, rows), :]
                new.append(jnp.where(inside, part[f, i] + vel[i] * side, 0.0))
            write(s, i, new, (new[0] - twice[s, i]) * new[1])


def middle_kernel(
    sy, sx, hy, hx, part, twice, halo, vel,
    near_out, near_image, packed,
    planes,
):
    scal = (sy, sx, hy, hx)
    rows = vel.shape[1]
    near_out[:, :, rows:, :] = jnp.zeros((4, R, MARGIN, planes.shape[3]), jnp.float32)

    def write(s, i, new, term):
        near_out[s, i, pl.ds(0, rows), :] = new[0]
        near_out[2 + s, i, pl.ds(0, rows), :] = new[1]
        near_image[i] = term if s == 0 else near_image[i] + term

    finish_near(scal, part, twice, halo, vel, planes, write)
    for f in range(4):
        pack_field(near_out, f, packed, scal, parity())


def second_far_kernel(
    sy, sx, hy, hx, depth, wave,
    before, near_cur, far_src, far_rcv, halo_src, halo_rcv, vel, delta, image_before,
    new_far, image_out,
    image, cur, matrix, xs, sems,
):
    scal = (sy, sx, hy, hx)
    par = parity()
    near, far = halves()
    layers, rows = vel.shape[0], vel.shape[1]
    base = lax.axis_index("slab") * layers
    src, rcv = pl.ds(0, 2), pl.ds(2, 2)
    own, halo = pl.ds(R + far, R), pl.ds((layers + R) * (1 - par), R)
    inner = pl.ds(MARGIN, rows)
    copies = copies_of([
        (far_src, cur.at[src, own, inner, :]),
        (far_rcv, cur.at[rcv, own, inner, :]),
        (near_cur.at[:, :, pl.ds(0, rows), :], cur.at[:, pl.ds(R + near, R), inner, :]),
        (halo_src, cur.at[src, halo, inner, :]),
        (halo_rcv, cur.at[rcv, halo, inner, :]),
    ], sems)
    clear(cur, None)
    band_matrix(matrix)
    wait(copies)
    x_part(cur, far, matrix, xs)
    refs = (cur, before.at[:, pl.ds(far, R)], vel.at[pl.ds(far, R)], delta.at[:, pl.ds(far, R)], xs)
    write = writer_far(scal, new_far.at[src], new_far.at[rcv], image, image_before)
    step_half(far, refs, scal, wave, depth, 1, base, write)
    used = R * rows
    image_out[:used] = image[...].reshape(used, image.shape[2])
    if image_out.shape[0] > used:
        image_out[used:] = jnp.zeros((image_out.shape[0] - used, image.shape[2]), jnp.float32)


def second_near_kernel(
    sy, sx, depth, wave,
    before, near_cur, far_src, far_rcv, vel, delta,
    near_part, near_twice,
    cur, matrix, xs, sems,
):
    scal = (sy, sx)
    par = parity()
    near, far = halves()
    layers, rows = vel.shape[0], vel.shape[1]
    base = lax.axis_index("slab") * layers
    inner = pl.ds(MARGIN, rows)
    copies = copies_of([
        (near_cur.at[:, :, pl.ds(0, rows), :], cur.at[:, pl.ds(R + near, R), inner, :]),
        (far_src, cur.at[pl.ds(0, 2), pl.ds(R + far, R), inner, :]),
        (far_rcv, cur.at[pl.ds(2, 2), pl.ds(R + far, R), inner, :]),
    ], sems)
    clear(cur, (layers + R) * par)
    band_matrix(matrix)
    wait(copies)
    x_part(cur, near, matrix, xs)
    refs = (cur, before.at[:, pl.ds(near, R)], vel.at[pl.ds(near, R)], delta.at[:, pl.ds(near, R)], xs)
    step_half(near, refs, scal, wave, depth, 1, base, writer_near(near_part, near_twice))


def last_kernel(
    sy, sx, hy, hx, part, twice, halo, vel, near_image,
    image, new_near,
    planes,
):
    scal = (sy, sx, hy, hx)

    def write(s, i, new, term):
        new_near[s, i] = new[0]
        new_near[2 + s, i] = new[1]
        image[i] = term + (near_image[i] if s == 0 else image[i])

    finish_near(scal, part, twice, halo, vel, planes, write)


def write_kernel(new_near, new_far, src_last, rcv_last, sems):
    near, far = halves()
    wait(copies_of([
        (new.at[pl.ds(2 * n, 2)], (src_last, rcv_last)[n].at[:, pl.ds(first, R)])
        for new, first in ((new_near, near), (new_far, far))
        for n in range(2)
    ], sems))


def image_kernel(near_a, near_b, far_a, far_b, out):
    near, far = halves()
    out[pl.ds(near, R)] = near_a[...] + near_b[...]
    used = R * out.shape[1]
    out[pl.ds(far, R)] = (far_a[:used] + far_b[:used]).reshape(R, *out.shape[1:])


def swap_a(block):
    count = lax.axis_size("slab")
    return lax.ppermute(block, "slab", [(i, i ^ 1) for i in range(count)])


def swap_b(block):
    count, groups = lax.axis_size("slab"), lax.axis_size("shots")
    pairs = []
    for i in range(count):
        for g in range(groups):
            to = (i, g ^ 1) if i in (0, count - 1) else (((i + 1) ^ 1) - 1, g)
            pairs.append((i * groups + g, to[0] * groups + to[1]))
    return lax.ppermute(block, ("slab", "shots"), pairs)


def swap_shots(block, turn, inner):
    count, groups = lax.axis_size("slab"), lax.axis_size("shots")
    pairs = []
    for i in range(count):
        is_inner = (i % 2 == 1) != (i >= count // 2)
        flip = 2 ** ((inner if is_inner else turn) + 1) - 1
        pairs += [(i * groups + g, i * groups + (g ^ flip)) for g in range(groups)]
    return lax.ppermute(block, ("slab", "shots"), pairs)


def shot_rounds(block, turn, inner):
    other = swap_shots(block, turn, inner)
    turn = 2
    while 2**turn < lax.axis_size("shots"):
        block = block + other
        other = swap_shots(block, turn, turn)
        turn += 1
    return block, other


def per_device(
    src_prev, src_cur, rcv_prev, rcv_cur, velocity, wavelet, residual_traces,
    source_depth, source_y, source_x, half_y, half_x, receiver_cell,
):
    layers, rows, cols = velocity.shape
    f32 = jnp.float32
    in_hbm = lambda x: pltpu.with_memory_space_constraint(x, pltpu.HBM)
    src_prev, src_cur, rcv_prev, rcv_cur, velocity = (
        in_hbm(x) for x in (src_prev, src_cur, rcv_prev, rcv_cur, velocity)
    )
    small_hbm = [
        in_hbm(x)
        for x in (source_y, source_x, half_y, half_x, source_depth, wavelet, receiver_cell, residual_traces)
    ]
    shape = jax.ShapeDtypeStruct
    half4 = shape((4, R, rows, cols), f32)
    half2 = shape((2, R, rows, cols), f32)
    half1 = shape((R, rows, cols), f32)
    far_block = shape((R * rows + SPARE, cols), f32)
    packed = shape((4 * R * PACK + TAIL, cols), f32)
    dma = lambda n: pltpu.SemaphoreType.DMA((n,))
    planes = (4, R, rows + MARGIN, cols)
    state = pltpu.VMEM((4, layers + 2 * R, rows + 2 * MARGIN, cols), f32)
    matrix = pltpu.VMEM((3 * cols, cols), jnp.bfloat16)
    xs = pltpu.VMEM((4, R, rows, cols), f32)

    to_b, *small, near_raw, far_raw = pl.pallas_call(
        pack_kernel,
        out_shape=(packed, *(shape(x.shape, x.dtype) for x in small_hbm), shape(planes, f32), half4),
        in_specs=[HBM] * 10,
        out_specs=(VMEM,) * 11,
        scratch_shapes=[dma(14)],
        compiler_params=params(),
        cost_estimate=cost(1 << 20, 1 << 20),
        name="pack_halo",
    )(*small_hbm, src_cur, rcv_cur)
    from_b = swap_b(to_b)
    halo_raw = swap_a(far_raw)
    scal = small[:6]

    far_src, far_rcv, far_image, near_part, near_twice, near_vel, before, vel, later = pl.pallas_call(
        first_kernel,
        out_shape=(half2, half2, half1, half4, half2, half1, shape((4, layers, rows, cols), f32), shape(velocity.shape, f32), shape((2, layers, rows, cols), f32)),
        in_specs=[VMEM] * 10 + [ANY] + [HBM] * 3,
        out_specs=(VMEM,) * 9,
        scratch_shapes=[state, pltpu.VMEM((4, layers, rows, cols), f32), pltpu.VMEM((2, layers, rows, cols), f32), matrix, xs, xs, dma(13)],
        compiler_params=params(),
        cost_estimate=cost(1 << 24, 1 << 25),
        name="first_step",
    )(*small, near_raw, far_raw, halo_raw, src_prev, rcv_prev, velocity)
    halo_src, halo_rcv = swap_a(far_src), swap_a(far_rcv)

    near_cur, near_image, to_b = pl.pallas_call(
        middle_kernel,
        out_shape=(shape(planes, f32), half1, packed),
        in_specs=[VMEM] * 8,
        out_specs=(VMEM,) * 3,
        scratch_shapes=[pltpu.VMEM(planes, f32)],
        compiler_params=params(),
        cost_estimate=cost(1 << 21, 1 << 26),
        name="first_step_near",
    )(*scal[:4], near_part, near_twice, from_b, near_vel)
    from_b = swap_b(to_b)

    new_far, far_image = pl.pallas_call(
        second_far_kernel,
        out_shape=(half4, far_block),
        in_specs=[VMEM] * 7 + [ANY] * 5 + [VMEM] * 3,
        out_specs=(VMEM, VMEM),
        scratch_shapes=[pltpu.VMEM((R, rows, cols), f32), state, matrix, xs, dma(5)],
        compiler_params=params(),
        cost_estimate=cost(1 << 23, 1 << 24),
        name="second_step_far",
    )(*scal, before, near_cur, far_src, far_rcv, halo_src, halo_rcv, vel, later, far_image)
    far_other = swap_shots(far_image, 1, 1)


    near_part, near_twice = pl.pallas_call(
        second_near_kernel,
        out_shape=(half4, half2),
        in_specs=[VMEM] * 5 + [ANY] * 3 + [VMEM] * 2,
        out_specs=(VMEM, VMEM),
        scratch_shapes=[state, matrix, xs, dma(3)],
        compiler_params=params(),
        cost_estimate=cost(1 << 23, 1 << 24),
        name="second_step_part",
    )(scal[0], scal[1], scal[4], scal[5], before, near_cur, far_src, far_rcv, vel, later)

    near_image, new_near = pl.pallas_call(
        last_kernel,
        out_shape=(half1, half4),
        in_specs=[VMEM] * 9,
        out_specs=(VMEM,) * 2,
        scratch_shapes=[pltpu.VMEM(planes, f32)],
        compiler_params=params(),
        cost_estimate=cost(1 << 21, 1 << 21),
        name="second_step_near",
    )(*scal[:4], near_part, near_twice, from_b, near_vel, near_image)
    near_other = swap_shots(near_image, 0, 1)
    near_image = near_image + near_other
    far_image = far_image + far_other
    near_a, near_b = shot_rounds(near_image, 1, 0)
    far_a, far_b = shot_rounds(far_image, 0, 0)

    src_last, rcv_last = pl.pallas_call(
        write_kernel,
        out_shape=(shape(src_cur.shape, f32),) * 2,
        in_specs=[VMEM, VMEM],
        out_specs=(HBM, HBM),
        scratch_shapes=[dma(4)],
        compiler_params=params(),
        cost_estimate=cost(1 << 10, 1 << 22),
        name="write_fields",
    )(new_near, new_far)

    image = pl.pallas_call(
        image_kernel,
        out_shape=shape((layers, rows, cols), f32),
        in_specs=[VMEM] * 4,
        out_specs=VMEM,
        compiler_params=params(),
        cost_estimate=cost(1 << 17, 1 << 20),
        name="image_sum",
    )(near_a, near_b, far_a, far_b)
    return src_last, rcv_last, image


def solution(mesh):
    return jax.shard_map(
        per_device,
        mesh=mesh,
        in_specs=(
            P("shots", "slab", None, None),
            P("shots", "slab", None, None),
            P("shots", "slab", None, None),
            P("shots", "slab", None, None),
            P("slab", None, None),
            P(None, "shots"),
            P(None, "shots", None),
            P("shots"),
            P("shots"),
            P("shots"),
            P("shots"),
            P("shots"),
            P("shots", None),
        ),
        out_specs=(
            P("shots", "slab", None, None),
            P("shots", "slab", None, None),
            P("slab", None, None),
        ),
        check_vma=False,
    )
```

```python
import functools

import jax
import jax.numpy as jnp
from jax import lax
from jax.experimental import pallas as pl
from jax.experimental.pallas import tpu as pltpu
from jax.sharding import PartitionSpec as P

STEPS = 2
COEF = (-205.0 / 72.0, 8.0 / 5.0, -1.0 / 5.0, 8.0 / 315.0, -1.0 / 560.0)
R = 4
HALF_Y, HALF_X = 21, 42
WIN_Y, WIN_X = 2 * HALF_Y + 1, 2 * HALF_X + 1
PACK = 29
LAST = 4 * R - 1
SHIFT = 3
REST = WIN_Y - PACK
SCALE = 5040.0
MARGIN = 8

SPARE = 16
VMEM = pl.BlockSpec(memory_space=pltpu.VMEM)
ANY = pl.BlockSpec(memory_space=pl.ANY)
HBM = pl.BlockSpec(memory_space=pltpu.HBM)


def params(**more):
    return pltpu.CompilerParams(vmem_limit_bytes=24 * 1024 * 1024, **more)


def cost(flops, nbytes):
    return pl.CostEstimate(flops=flops, bytes_accessed=nbytes, transcendentals=0)


def parity():
    return lax.rem(lax.axis_index("slab"), 2)


def halves():
    par = parity()
    return par * R, R - par * R


def lanes(shape):
    return lax.broadcasted_iota(jnp.int32, shape, 1)


def sublanes(shape):
    return lax.broadcasted_iota(jnp.int32, shape, 0)


def band(scal, s, shape):
    sy, sx, hy, hx = (ref[s] for ref in scal)
    return (jnp.abs(sublanes(shape) - sy) <= hy) & (jnp.abs(lanes(shape) - sx) <= hx)


def inside_columns(col0, shape):
    lane = lanes(shape)
    return (lane >= col0) & (lane < col0 + WIN_X)


def pack(planes, f, i, row0, col0):
    main = planes[f, i, pl.ds(row0, 32), :]
    left = pltpu.roll(planes[f, i, pl.ds(row0 + PACK, 16), :], WIN_X, 1)
    right = pltpu.roll(planes[f, i, pl.ds(row0 + PACK - REST + 8, 24), :], HALF_X, 1)
    left = jnp.concatenate([left, right[8:]], 0)
    right = jnp.concatenate([right[:8], right], 0)
    spare = jnp.where(sublanes(main.shape) < REST, left, right)
    return jnp.where(inside_columns(col0, main.shape), main, spare)


def pack_field(planes, f, out, scal, par):
    row0 = scal[0][f % 2] - HALF_Y
    col0 = scal[1][f % 2] - HALF_X
    for d in reversed(range(R)):
        i = d + par * (R - 1 - 2 * d)
        n = f * R + d
        block = pack(planes, f, i, row0, col0)
        if n == LAST:
            out[LAST * PACK - SHIFT :] = pltpu.roll(block, SHIFT, 0)
        else:
            out[pl.ds(n * PACK, PACK), :] = block[:PACK]


def unpack_planes(packed, planes, scal):
    cols = packed.shape[1]
    for f in range(4):
        row0 = scal[0][f % 2] - HALF_Y
        col0 = scal[1][f % 2] - HALF_X
        for e in range(R):
            n = f * R + e
            if n == LAST:
                block = packed[LAST * PACK - SHIFT :]
                rows = block.shape[0]
                main = pltpu.roll(block, rows - SHIFT, 0)[:PACK]
                left = main[:REST]
                right = pltpu.roll(block, rows - SHIFT - REST, 0)[:REST]
            else:
                main = packed[pl.ds(n * PACK, PACK), :]
                left = packed[pl.ds(n * PACK, REST), :]
                right = packed[pl.ds(n * PACK + REST, REST), :]
            planes[f, e, pl.ds(row0, PACK), :] = main
            left = pltpu.roll(left, cols - WIN_X, 1)
            right = pltpu.roll(right, cols - HALF_X, 1)
            rest = jnp.where(lanes(left.shape) < col0 + (cols - WIN_X), left, right)
            planes[f, e, pl.ds(row0 + PACK, REST), :] = rest


def copies_of(pairs, sems):
    copies = [pltpu.make_async_copy(a, b, sems.at[n]) for n, (a, b) in enumerate(pairs)]
    for copy in copies:
        copy.start()
    return copies


def wait(copies):
    for copy in copies:
        copy.wait()


def pack_kernel(*refs):
    small_in, (src, rcv, out), small, (planes, far_raw, sems) = refs[:8], refs[8:11], refs[11:19], refs[19:]
    near, far = halves()
    rows = src.shape[2]
    pairs = []
    for f in range(4):
        ref = (src, rcv)[f // 2].at[f % 2]
        pairs.append((ref.at[pl.ds(near, R)], planes.at[f, :, pl.ds(0, rows), :]))
    pairs += list(zip(small_in, small))
    for n, ref in enumerate((src, rcv)):
        pairs.append((ref.at[:, pl.ds(far, R)], far_raw.at[pl.ds(2 * n, 2)]))
    copies = copies_of(pairs, sems)
    planes[:, :, rows:, :] = jnp.zeros((4, R, MARGIN, planes.shape[3]), jnp.float32)
    wait(copies[:6])
    for f in range(4):
        pack_field(planes, f, out, small[:2], parity())
    wait(copies[6:])


def band_matrix(out):
    cols = out.shape[1]
    apart = jnp.abs(sublanes((cols, cols)) - lanes((cols, cols)))
    weights = jnp.zeros((cols, cols), jnp.float32)
    for k in range(1, R + 1):
        weights = jnp.where(apart == k, round(COEF[k] * SCALE) * 1.0, weights)
    for n in range(3):
        out[pl.ds(n * cols, cols)] = weights.astype(jnp.bfloat16)


def x_part(cur, first, matrix, out):
    rows, cols = out.shape[2], out.shape[3]
    for f in range(4):
        rest = cur[f, pl.ds(first + R, R), pl.ds(MARGIN, rows), :].reshape(R * rows, cols)
        parts = []
        for _ in range(3):
            parts.append(rest.astype(jnp.bfloat16))
            rest = rest - parts[-1].astype(jnp.float32)
        total = lax.dot_general(
            jnp.concatenate(parts, 1),
            matrix[...],
            (((1,), (0,)), ((), ())),
            preferred_element_type=jnp.float32,
        )
        out[f] = total.reshape(R, rows, cols)


def laplace(cur, xs, f, i, slot, rows):
    at = lambda layer, row: cur[f, layer, pl.ds(MARGIN + row, rows), :]
    total = 3.0 * COEF[0] * at(slot, 0) + (1.0 / SCALE) * xs[f, i]
    for k in range(1, R + 1):
        side_z = at(slot - k, 0) + at(slot + k, 0)
        side_y = at(slot, -k) + at(slot, k)
        total = total + COEF[k] * (side_z + side_y)
    return total


def inject(cells, traces, first, outs):
    shots, layers, rows, cols = outs[0].shape
    count = cells.shape[1]
    for s in range(shots):
        flat = cells[pl.ds(s, 1), :]
        line = lax.div(flat, cols)
        col = flat - line * cols
        line = line - first * rows
        spot = sublanes((layers * rows, count)) == line
        spot = jnp.where(spot, 1.0, 0.0).astype(jnp.bfloat16)
        here = sublanes((cols, count)) == col
        value = jnp.concatenate(
            [jnp.where(here, traces[step, pl.ds(s, 1), :], 0.0) for step in range(STEPS)], 0
        )
        total = None
        for _ in range(3):
            part = value.astype(jnp.bfloat16)
            value = value - part.astype(jnp.float32)
            term = lax.dot_general(
                spot, part, (((1,), (1,)), ((), ())), preferred_element_type=jnp.float32
            )
            total = term if total is None else total + term
        for step, out in enumerate(outs):
            out[s] = total[:, step * cols : (step + 1) * cols].reshape(layers, rows, cols)


def clear(ref, layers):
    fields, slots, tall, cols = ref.shape
    ref[:, :, :MARGIN, :] = jnp.zeros((fields, slots, MARGIN, cols), jnp.float32)
    ref[:, :, tall - MARGIN :, :] = jnp.zeros((fields, slots, MARGIN, cols), jnp.float32)
    if layers is not None:
        ref[:, pl.ds(layers, R), :, :] = jnp.zeros((fields, R, tall, cols), jnp.float32)


def step_half(first, refs, scal, wave, depth, step, base, write):
    cur, prev, vel, delta, xs = refs
    rows = vel.shape[1]
    for s in range(2):
        spot = (sublanes(vel.shape[1:]) == scal[0][s]) & (lanes(vel.shape[1:]) == scal[1][s])
        here = depth[s] - base

        def layer(i, _):
            p = first + i
            amount = jnp.where(here == p, wave[step, s], 0.0)
            out = []
            for f in (s, 2 + s):
                twice = 2.0 * cur[f, p + R, pl.ds(MARGIN, rows), :] - prev[f, i]
                new = twice + vel[i] * laplace(cur, xs, f, i, p + R, rows)
                if f < 2:
                    new = new + jnp.where(spot, amount, 0.0)
                else:
                    new = new + delta[s, i]
                out.append((twice, new))
            write(s, i, out)
            return 0

        lax.fori_loop(0, R, layer, 0, unroll=True)


def writer_far(scal, new_src, new_rcv, image, before):
    shape = image.shape[1:]

    def write(s, i, out):
        inside = band(scal, s, shape)
        new = [jnp.where(inside, n, 0.0) for _, n in out]
        new_src[s, i] = new[0]
        new_rcv[s, i] = new[1]
        term = (new[0] - out[0][0]) * new[1]
        if s == 0:
            image[i] = term if before is None else term + before[i]
        else:
            image[i] = image[i] + term

    return write


def writer_near(part, twice):
    def write(s, i, out):
        part[s, i] = out[0][1]
        part[2 + s, i] = out[1][1]
        twice[s, i] = out[0][0]

    return write


def first_kernel(
    sy, sx, hy, hx, depth, wave, cells, traces, planes, far_raw, halo_raw,
    src_prev, rcv_prev, vel_in,
    src_out, rcv_out, far_image, near_part, near_twice, near_vel, before, vel, later,
    cur, prev, delta, matrix, xs_near, xs_far, sems,
):
    scal = (sy, sx, hy, hx)
    par = parity()
    near, far = halves()
    layers, rows = vel_in.shape[0], vel_in.shape[1]
    base = lax.axis_index("slab") * layers
    inner = pl.ds(MARGIN, rows)
    near_raw = planes.at[:, :, pl.ds(0, rows), :]
    halo = (layers + R) * (1 - par)
    fields = (pl.ds(0, 2), pl.ds(2, 2))
    pairs = [
        (near_raw, cur.at[:, pl.ds(R + near, R), inner, :]),
        (near_raw, before.at[:, pl.ds(near, R)]),
    ]
    pairs += [
        (far_raw, cur.at[:, pl.ds(R + far, R), inner, :]),
        (far_raw, before.at[:, pl.ds(far, R)]),
        (halo_raw, cur.at[:, pl.ds(halo, R), inner, :]),
    ]
    pairs.append((vel_in, vel))
    for first in (near, far):
        for ref, n in ((src_prev, 0), (rcv_prev, 1)):
            pairs.append((ref.at[:, pl.ds(first, R)], prev.at[fields[n], pl.ds(first, R)]))
    copies = copies_of(pairs, sems)
    clear(cur, (layers + R) * par)
    band_matrix(matrix)
    inject(cells, traces, base, (delta, later))
    wait(copies[:5])
    x_part(cur, near, matrix, xs_near)
    x_part(cur, far, matrix, xs_far)
    wait(copies[5:8])
    has = jnp.where((base == 0) | (lax.axis_index("slab") == lax.axis_size("slab") - 1), 0.0, 1.0)
    near_vel[...] = vel[pl.ds(near, R)] * has

    def half_step(first, xs, write):
        refs = (cur, prev.at[:, pl.ds(first, R)], vel.at[pl.ds(first, R)], delta.at[:, pl.ds(first, R)], xs)
        step_half(first, refs, scal, wave, depth, 0, base, write)

    half_step(near, xs_near, writer_near(near_part, near_twice))
    wait(copies[8:])
    half_step(far, xs_far, writer_far(scal, src_out, rcv_out, far_image, None))


def finish_near(scal, part, twice, halo, vel, planes, write):
    par = parity()
    rows, cols = vel.shape[1], vel.shape[2]
    unpack_planes(halo, planes, scal)
    for s in range(2):
        inside = band(scal, s, (rows, cols))
        for d in range(R):
            i = d + par * (R - 1 - 2 * d)
            new = []
            for f in (s, 2 + s):
                side = COEF[d + 1] * planes[f, 0, pl.ds(0, rows), :]
                for k in range(d + 2, R + 1):
                    side = side + COEF[k] * planes[f, k - d - 1, pl.ds(0, rows), :]
                new.append(jnp.where(inside, part[f, i] + vel[i] * side, 0.0))
            write(s, i, new, (new[0] - twice[s, i]) * new[1])


def middle_kernel(
    sy, sx, hy, hx, part, twice, halo, vel,
    near_out, near_image, packed,
    planes,
):
    scal = (sy, sx, hy, hx)
    rows = vel.shape[1]
    near_out[:, :, rows:, :] = jnp.zeros((4, R, MARGIN, planes.shape[3]), jnp.float32)

    def write(s, i, new, term):
        near_out[s, i, pl.ds(0, rows), :] = new[0]
        near_out[2 + s, i, pl.ds(0, rows), :] = new[1]
        near_image[i] = term if s == 0 else near_image[i] + term

    finish_near(scal, part, twice, halo, vel, planes, write)
    for f in range(4):
        pack_field(near_out, f, packed, scal, parity())


def second_far_kernel(
    sy, sx, hy, hx, depth, wave,
    before, near_cur, far_src, far_rcv, halo_src, halo_rcv, vel, delta, image_before,
    new_far, image_out,
    image, cur, matrix, xs, sems,
):
    scal = (sy, sx, hy, hx)
    par = parity()
    near, far = halves()
    layers, rows = vel.shape[0], vel.shape[1]
    base = lax.axis_index("slab") * layers
    src, rcv = pl.ds(0, 2), pl.ds(2, 2)
    own, halo = pl.ds(R + far, R), pl.ds((layers + R) * (1 - par), R)
    inner = pl.ds(MARGIN, rows)
    copies = copies_of([
        (far_src, cur.at[src, own, inner, :]),
        (far_rcv, cur.at[rcv, own, inner, :]),
        (near_cur.at[:, :, pl.ds(0, rows), :], cur.at[:, pl.ds(R + near, R), inner, :]),
        (halo_src, cur.at[src, halo, inner, :]),
        (halo_rcv, cur.at[rcv, halo, inner, :]),
    ], sems)
    clear(cur, None)
    band_matrix(matrix)
    wait(copies)
    x_part(cur, far, matrix, xs)
    refs = (cur, before.at[:, pl.ds(far, R)], vel.at[pl.ds(far, R)], delta.at[:, pl.ds(far, R)], xs)
    write = writer_far(scal, new_far.at[src], new_far.at[rcv], image, image_before)
    step_half(far, refs, scal, wave, depth, 1, base, write)
    used = R * rows
    image_out[:used] = image[...].reshape(used, image.shape[2])
    if image_out.shape[0] > used:
        image_out[used:] = jnp.zeros((image_out.shape[0] - used, image.shape[2]), jnp.float32)


def second_near_kernel(
    sy, sx, depth, wave,
    before, near_cur, far_src, far_rcv, vel, delta,
    near_part, near_twice,
    cur, matrix, xs, sems,
):
    scal = (sy, sx)
    par = parity()
    near, far = halves()
    layers, rows = vel.shape[0], vel.shape[1]
    base = lax.axis_index("slab") * layers
    inner = pl.ds(MARGIN, rows)
    copies = copies_of([
        (near_cur.at[:, :, pl.ds(0, rows), :], cur.at[:, pl.ds(R + near, R), inner, :]),
        (far_src, cur.at[pl.ds(0, 2), pl.ds(R + far, R), inner, :]),
        (far_rcv, cur.at[pl.ds(2, 2), pl.ds(R + far, R), inner, :]),
    ], sems)
    clear(cur, (layers + R) * par)
    band_matrix(matrix)
    wait(copies)
    x_part(cur, near, matrix, xs)
    refs = (cur, before.at[:, pl.ds(near, R)], vel.at[pl.ds(near, R)], delta.at[:, pl.ds(near, R)], xs)
    step_half(near, refs, scal, wave, depth, 1, base, writer_near(near_part, near_twice))


def last_kernel(
    sy, sx, hy, hx, part, twice, halo, vel, near_image,
    image, new_near,
    planes,
):
    scal = (sy, sx, hy, hx)

    def write(s, i, new, term):
        new_near[s, i] = new[0]
        new_near[2 + s, i] = new[1]
        image[i] = term + (near_image[i] if s == 0 else image[i])

    finish_near(scal, part, twice, halo, vel, planes, write)


def write_kernel(new_near, new_far, src_last, rcv_last, sems):
    near, far = halves()
    wait(copies_of([
        (new.at[pl.ds(2 * n, 2)], (src_last, rcv_last)[n].at[:, pl.ds(first, R)])
        for new, first in ((new_near, near), (new_far, far))
        for n in range(2)
    ], sems))


def image_kernel(near_a, near_b, far_a, far_b, out, sums, sems):
    near, far = halves()
    used = R * out.shape[1]
    copies = [
        pltpu.make_async_copy(sums.at[n], out.at[pl.ds(first, R)], sems.at[n])
        for n, first in enumerate((far, near))
    ]
    sums[0] = (far_a[:used] + far_b[:used]).reshape(R, *out.shape[1:])
    copies[0].start()
    sums[1] = near_a[...] + near_b[...]
    copies[1].start()
    wait(copies)


def swap_a(block):
    count = lax.axis_size("slab")
    return lax.ppermute(block, "slab", [(i, i ^ 1) for i in range(count)])


def swap_b(block):
    count, groups = lax.axis_size("slab"), lax.axis_size("shots")
    pairs = []
    for i in range(count):
        for g in range(groups):
            to = (i, g ^ 1) if i in (0, count - 1) else (((i + 1) ^ 1) - 1, g)
            pairs.append((i * groups + g, to[0] * groups + to[1]))
    return lax.ppermute(block, ("slab", "shots"), pairs)


def swap_shots(block, turn, inner):
    count, groups = lax.axis_size("slab"), lax.axis_size("shots")
    pairs = []
    for i in range(count):
        is_inner = (i % 2 == 1) != (i >= count // 2)
        flip = 2 ** ((inner if is_inner else turn) + 1) - 1
        pairs += [(i * groups + g, i * groups + (g ^ flip)) for g in range(groups)]
    return lax.ppermute(block, ("slab", "shots"), pairs)


def shot_rounds(block, turn, inner):
    other = swap_shots(block, turn, inner)
    turn = 2
    while 2**turn < lax.axis_size("shots"):
        block = block + other
        other = swap_shots(block, turn, turn)
        turn += 1
    return block, other


def per_device(
    src_prev, src_cur, rcv_prev, rcv_cur, velocity, wavelet, residual_traces,
    source_depth, source_y, source_x, half_y, half_x, receiver_cell,
):
    layers, rows, cols = velocity.shape
    f32 = jnp.float32
    in_hbm = lambda x: pltpu.with_memory_space_constraint(x, pltpu.HBM)
    src_prev, src_cur, rcv_prev, rcv_cur, velocity = (
        in_hbm(x) for x in (src_prev, src_cur, rcv_prev, rcv_cur, velocity)
    )
    small_hbm = [
        in_hbm(x)
        for x in (source_y, source_x, half_y, half_x, source_depth, wavelet, receiver_cell, residual_traces)
    ]
    shape = jax.ShapeDtypeStruct
    half4 = shape((4, R, rows, cols), f32)
    half2 = shape((2, R, rows, cols), f32)
    half1 = shape((R, rows, cols), f32)
    far_block = shape((R * rows + SPARE, cols), f32)
    packed = shape((4 * R * PACK, cols), f32)
    dma = lambda n: pltpu.SemaphoreType.DMA((n,))
    planes = (4, R, rows + MARGIN, cols)
    state = pltpu.VMEM((4, layers + 2 * R, rows + 2 * MARGIN, cols), f32)
    matrix = pltpu.VMEM((3 * cols, cols), jnp.bfloat16)
    xs = pltpu.VMEM((4, R, rows, cols), f32)

    to_b, *small, near_raw, far_raw = pl.pallas_call(
        pack_kernel,
        out_shape=(packed, *(shape(x.shape, x.dtype) for x in small_hbm), shape(planes, f32), half4),
        in_specs=[HBM] * 10,
        out_specs=(VMEM,) * 11,
        scratch_shapes=[dma(14)],
        compiler_params=params(),
        cost_estimate=cost(1 << 20, 1 << 20),
        name="pack_halo",
    )(*small_hbm, src_cur, rcv_cur)
    from_b = swap_b(to_b)
    halo_raw = swap_a(far_raw)
    scal = small[:6]

    far_src, far_rcv, far_image, near_part, near_twice, near_vel, before, vel, later = pl.pallas_call(
        first_kernel,
        out_shape=(half2, half2, half1, half4, half2, half1, shape((4, layers, rows, cols), f32), shape(velocity.shape, f32), shape((2, layers, rows, cols), f32)),
        in_specs=[VMEM] * 10 + [ANY] + [HBM] * 3,
        out_specs=(VMEM,) * 9,
        scratch_shapes=[state, pltpu.VMEM((4, layers, rows, cols), f32), pltpu.VMEM((2, layers, rows, cols), f32), matrix, xs, xs, dma(13)],
        compiler_params=params(),
        cost_estimate=cost(1 << 24, 1 << 25),
        name="first_step",
    )(*small, near_raw, far_raw, halo_raw, src_prev, rcv_prev, velocity)
    halo_src, halo_rcv = swap_a(far_src), swap_a(far_rcv)

    near_cur, near_image, to_b = pl.pallas_call(
        middle_kernel,
        out_shape=(shape(planes, f32), half1, packed),
        in_specs=[VMEM] * 8,
        out_specs=(VMEM,) * 3,
        scratch_shapes=[pltpu.VMEM(planes, f32)],
        compiler_params=params(),
        cost_estimate=cost(1 << 21, 1 << 26),
        name="first_step_near",
    )(*scal[:4], near_part, near_twice, from_b, near_vel)
    from_b = swap_b(to_b)

    new_far, far_image = pl.pallas_call(
        second_far_kernel,
        out_shape=(half4, far_block),
        in_specs=[VMEM] * 7 + [ANY] * 5 + [VMEM] * 3,
        out_specs=(VMEM, VMEM),
        scratch_shapes=[pltpu.VMEM((R, rows, cols), f32), state, matrix, xs, dma(5)],
        compiler_params=params(),
        cost_estimate=cost(1 << 23, 1 << 24),
        name="second_step_far",
    )(*scal, before, near_cur, far_src, far_rcv, halo_src, halo_rcv, vel, later, far_image)
    far_other = swap_shots(far_image, 1, 1)


    near_part, near_twice = pl.pallas_call(
        second_near_kernel,
        out_shape=(half4, half2),
        in_specs=[VMEM] * 5 + [ANY] * 3 + [VMEM] * 2,
        out_specs=(VMEM, VMEM),
        scratch_shapes=[state, matrix, xs, dma(3)],
        compiler_params=params(),
        cost_estimate=cost(1 << 23, 1 << 24),
        name="second_step_part",
    )(scal[0], scal[1], scal[4], scal[5], before, near_cur, far_src, far_rcv, vel, later)

    near_image, new_near = pl.pallas_call(
        last_kernel,
        out_shape=(half1, half4),
        in_specs=[VMEM] * 9,
        out_specs=(VMEM,) * 2,
        scratch_shapes=[pltpu.VMEM(planes, f32)],
        compiler_params=params(),
        cost_estimate=cost(1 << 21, 1 << 21),
        name="second_step_near",
    )(*scal[:4], near_part, near_twice, from_b, near_vel, near_image)
    near_other = swap_shots(near_image, 0, 1)
    near_image = near_image + near_other
    far_image = far_image + far_other
    near_a, near_b = shot_rounds(near_image, 1, 0)
    far_a, far_b = shot_rounds(far_image, 0, 0)

    src_last, rcv_last = pl.pallas_call(
        write_kernel,
        out_shape=(shape(src_cur.shape, f32),) * 2,
        in_specs=[VMEM, VMEM],
        out_specs=(HBM, HBM),
        scratch_shapes=[dma(4)],
        compiler_params=params(),
        cost_estimate=cost(1 << 10, 1 << 22),
        name="write_fields",
    )(new_near, new_far)

    image = pl.pallas_call(
        image_kernel,
        out_shape=shape((layers, rows, cols), f32),
        in_specs=[VMEM] * 4,
        out_specs=HBM,
        scratch_shapes=[pltpu.VMEM((2, R, rows, cols), f32), dma(2)],
        compiler_params=params(),
        cost_estimate=cost(1 << 17, 1 << 20),
        name="image_sum",
    )(near_a, near_b, far_a, far_b)
    return src_last, rcv_last, image


def solution(mesh):
    return jax.shard_map(
        per_device,
        mesh=mesh,
        in_specs=(
            P("shots", "slab", None, None),
            P("shots", "slab", None, None),
            P("shots", "slab", None, None),
            P("shots", "slab", None, None),
            P("slab", None, None),
            P(None, "shots"),
            P(None, "shots", None),
            P("shots"),
            P("shots"),
            P("shots"),
            P("shots"),
            P("shots"),
            P("shots", None),
        ),
        out_specs=(
            P("shots", "slab", None, None),
            P("shots", "slab", None, None),
            P("slab", None, None),
        ),
        check_vma=False,
    )
```
